512 devices in a mesh: prow: 16 (over x, y), pcol: 32 (over z, core).
Axes of the slice: x: 4, y: 4, z: 16, core: 2. Of those that a mesh axis runs over, the one named last changes fastest.
Arguments:
- matrix: float32 [4096, 32768], P('prow', 'pcol'), may hold values from -6 to 6
- lpanel: float32 [4096, 256], P(('prow', 'pcol')), may hold values from -0.375 to 0.375
- linv: float32 [256, 256], replicated, as said below
- pivots: int32 [256], replicated, may hold values from 256 to 4095, as said below
- weights: float32 [2, 4096], P(None, 'prow'), may hold values from -0.09375 to 0.09375
Outputs:
- updated: float32 [4096, 32768], P('prow', 'pcol')
- checks: float32 [2, 32768], P(None, 'pcol')
The draws below stay inside these ranges and needn't reach their ends.
Inputs may be any that keep to these rules, and one draw needn't show every extreme that they name: `pivots`: distinct row indices outside the first 256 rows; 256 and 4095 both occur. `linv`: unit lower triangular.
All inputs are finite; a program needn't handle non-finite values.
Results may differ from the reference program's by a relative error of at most 0.000071.
Values sent between devices are 32-bit elements; how exact they have to be, the bound alone decides.
A program may use at most 64 MiB of HBM per device.

```python
import math
import jax
import jax.numpy as jnp
from jax import lax

NB = 256
NCS = 2
M = 4096
NCOLS = 32768


def draw_linv(key, part):
    key = jax.random.fold_in(key, 11)
    noise = jax.random.normal(key, (NB, NB), jnp.float32) * 0.7
    row_ids = lax.broadcasted_iota(jnp.int32, (NB, NB), 0)
    col_ids = lax.broadcasted_iota(jnp.int32, (NB, NB), 1)
    return jnp.where(row_ids > col_ids, noise / math.sqrt(NB), jnp.where(row_ids == col_ids, 1.0, 0.0)).astype(jnp.float32)


def draw_pivots(key, part):
    key = jax.random.fold_in(key, 23)
    keys = jax.random.split(key, 3)
    picks = jax.random.permutation(keys[0], M - NB - 2)[:NB] + NB + 1
    first_slot = jax.random.randint(keys[1], (), 0, NB)
    second_slot = (first_slot + jax.random.randint(keys[2], (), 1, NB)) % NB
    picks = picks.at[first_slot].set(M - 1).at[second_slot].set(NB)
    return picks.astype(jnp.int32)


def shard_levels(rng, shape, shards, smallest, high):
    factor_of, own = 1.0, jax.random.fold_in(rng, 6)
    for dim, shards_of in shards:
        steps = jnp.exp(jax.random.uniform(jax.random.fold_in(own, dim), (shards_of,), jnp.float32, smallest / len(shards), high / len(shards)))
        factor_of = factor_of * jnp.repeat(steps, shape[dim] // shards_of).reshape([-1 if axis == dim else 1 for axis in range(len(shape))])
    return factor_of


def gaussian(own_key, shape, deviation, most, cuts=(), held_as=jnp.bfloat16):
    gain = shard_levels(own_key, shape, cuts, -0.22, 0.18) if cuts else 1.0
    drawn = jax.random.normal(own_key, shape, jnp.float32) * deviation * gain
    return jnp.minimum(jnp.maximum(drawn, -most), most).astype(held_as)


def setup_inputs(seed: int = 0) -> dict:
    streams_of = jax.random.split(jax.random.key(seed), 6)
    matrix = gaussian(streams_of[0], (M, NCOLS), 1.0, 6.0, ((0, 16), (1, 32)), jnp.float32)
    lpanel = gaussian(streams_of[1], (M, NB), NB ** -0.5, 0.375, ((0, 512),), jnp.float32)
    linv = draw_linv(jax.random.fold_in(streams_of[5], 71), 0)
    pivots = draw_pivots(jax.random.fold_in(streams_of[5], 71), 0)
    weights = gaussian(streams_of[4], (NCS, M), M ** -0.5, 0.09375, ((1, 16),), jnp.float32)
    return {"matrix": matrix, "lpanel": lpanel, "linv": linv, "pivots": pivots, "weights": weights}


def reference(matrix, lpanel, linv, pivots, weights):
    top_block = matrix[:NB]
    pivot_rows = matrix[pivots]
    swapped = matrix.at[pivots].set(top_block).at[:NB].set(pivot_rows)
    solved = jnp.dot(linv, pivot_rows, precision=lax.Precision.HIGHEST, preferred_element_type=jnp.float32)
    lower = swapped[NB:] - jnp.dot(lpanel[NB:], solved, precision=lax.Precision.HIGHEST, preferred_element_type=jnp.float32)
    updated = jnp.concatenate([solved, lower], axis=0)
    checks = jnp.dot(weights, updated, precision=lax.Precision.HIGHEST, preferred_element_type=jnp.float32)
    return updated, checks
```

```python
import functools
import types

import jax
import jax.numpy as jnp
from jax import lax
from jax.experimental import pallas as pl
from jax.experimental.pallas import tpu as pltpu
from jax.sharding import PartitionSpec as P

MESH = pl.DeviceIdType.MESH
HIGHEST = lax.Precision.HIGHEST
NB = 256
SIDE = 4
W = 256
NCH = 4
COPIES = 8
QUARTER = NB // SIDE


def dot(a, b):
    return jnp.dot(a, b, precision=HIGHEST, preferred_element_type=jnp.float32)


def bdot(a, b):
    return jnp.dot(a, b, preferred_element_type=jnp.float32)


def split(value):
    high = value.astype(jnp.bfloat16)
    return high, (value - high.astype(jnp.float32)).astype(jnp.bfloat16)


def few_rows(rows, wide):
    pair = jnp.concatenate([piece.astype(jnp.float32) for piece in split(rows)], axis=0).astype(jnp.bfloat16)
    product = sum(bdot(pair, piece) for piece in reversed(wide))
    return product[0:8] + product[8:16]


def rows_of(start, size):
    return pl.ds(pl.multiple_of(start, size), size)


def kernel(
    nz,
    m_hbm, l_hbm, linv_hbm, piv_hbm, w_hbm,
    out_ref, chk_ref,
    mat, contrib, owners, owners_b, linv, piv, w8, own_rows, lbuf, vbuf, usum,
    up1, t1s, v1s, up2, esend, slots,
    linv_high, linv_low, picks, places, factor_high, factor_low, rows_high, rows_low, wp_x, wp_y, sums_x, sums_y, totals,
    load_sem, mat_sem,
    su, ru, s2, r2, sd, rd,
    zs, zr, us, ur, cs, cr,
):
    prow, pcol = lax.axis_index("prow"), lax.axis_index("pcol")
    x, y = prow // SIDE, prow % SIDE
    z, core = pcol // 2, pcol % 2
    top = prow == 0

    x_peers = [(lax.rem(x + d, SIDE) * SIDE + y, pcol) for d in (1, 2, 3)]
    y_peers = [(x * SIDE + lax.rem(y + d, SIDE), pcol) for d in (1, 2, 3)]
    far_first = sorted(range(1, nz), key=lambda d: -min(d, nz - d))
    line = [lax.rem(z + d, nz) * 2 for d in far_first]
    z_peers = [(prow, column + 1) for column in line]
    plane_peers = [(lax.rem(prow + d, SIDE * SIDE), pcol) for d in range(1, SIDE * SIDE)]
    twin = (prow, z * 2 + 1 - core)

    w8[...] = jnp.zeros_like(w8)
    loads = [
        pltpu.make_async_copy(piv_hbm, piv, load_sem.at[0]),
        pltpu.make_async_copy(w_hbm, w8.at[pl.ds(0, 2)], load_sem.at[1]),
        pltpu.make_async_copy(l_hbm, own_rows, load_sem.at[2]),
        pltpu.make_async_copy(linv_hbm, linv, load_sem.at[3]),
    ]
    for copy in loads[:2]:
        copy.start()

    def chunk_cols(n):
        return pl.ds(pl.multiple_of((n % 2) * 2 * W + (n // 2) * W, W), W)

    def mat_load(n):
        cols = chunk_cols(n)
        return pltpu.make_async_copy(m_hbm.at[:, cols], mat.at[:, cols], mat_sem.at[n])

    for n in range(NCH):
        mat_load(n).start()
    for copy in loads[2:]:
        copy.start()

    barrier = pltpu.get_barrier_semaphore()

    def greet(peer):
        pl.semaphore_signal(barrier, inc=1, device_id=peer, device_id_type=MESH)

    for row, _ in x_peers + y_peers:
        greet((row, z * 2))

    @pl.when(core == 1)
    def _():
        greet(twin)
        for column in line:
            greet((prow, column + 1))

    def remote(src, dst, send_sem, recv_sem, peer):
        return pltpu.make_async_remote_copy(
            src_ref=src, dst_ref=dst, send_sem=send_sem, recv_sem=recv_sem,
            device_id=peer, device_id_type=MESH,
        )

    def begin(copies):
        for copy in copies:
            copy.start()

    def left(copies):
        for copy in copies:
            copy.wait_send()

    def landed(copies):
        for copy in copies:
            copy.wait_recv()

    def on(which):
        return pl.when(core == which)

    loads[0].wait()
    loads[1].wait()
    base = prow * NB
    row_ids = lax.broadcasted_iota(jnp.int32, (NB, NB), 0)
    lane_ids = lax.broadcasted_iota(jnp.int32, (NB, NB), 1)
    piv_cols = jnp.transpose(jnp.broadcast_to(piv[...], (NB, NB)))
    pick = jnp.where(piv_cols - base == lane_ids, 1.0, 0.0)
    picks[pl.ds(0, NB), :] = pick.astype(jnp.bfloat16)
    keep_row = 1.0 - jnp.sum(pick, axis=0, keepdims=True)
    kept = jnp.concatenate([piece.astype(jnp.float32) for piece in split(w8[...] * keep_row)], axis=0)
    picks[pl.ds(NB, 16), :] = kept.astype(jnp.bfloat16)

    def ring_of(half):
        a, b = (x, y) if half == 0 else (y, x)

        def place(a, b):
            return a * SIDE + b if half == 0 else b * SIDE + a

        outer = {d: lax.rem(a + d, SIDE) for d in (0, 1, 2, 3)}
        inner = {d: lax.rem(b + d, SIDE) for d in (1, 2, 3)}
        return types.SimpleNamespace(
            half=half, a=a, b=b, outer=outer, inner=inner,
            who={d: place(outer[d], b) for d in outer},
            to={d: (place(outer[d], b), pcol) for d in outer},
            to_inner={d: (place(a, inner[d]), pcol) for d in inner},
            rows={d: rows_of(outer[d] * QUARTER, QUARTER) for d in outer},
        )

    rings = ring_of(0), ring_of(1)

    def up_outer(n):
        r = rings[n % 2]
        return [
            remote(
                contrib.at[r.rows[d], chunk_cols(n)], up1.at[n, d - 1], su.at[n, d - 1], ru.at[n, d - 1], r.to[d])
            for d in (1, 2, 3)
        ]

    def inner(n):
        r = rings[n % 2]
        return [
            remote(
                v1s.at[n], up2.at[n, d - 1], s2.at[n, d - 1], r2.at[n, d - 1], r.to_inner[d])
            for d in (1, 2, 3)
        ]

    def down_outer(n):
        r = rings[n % 2]
        return [
            remote(
                esend.at[n, d - 1], slots.at[r.rows[0], chunk_cols(n)], sd.at[n, d - 1], rd.at[n, d - 1], r.to[d])
            for d in (1, 2, 3)
        ]

    wp_row, wp_column, wp = wp_x.at[x], wp_y.at[y], wp_x.at[SIDE]
    sums_row, sums_column = sums_x.at[x], sums_y.at[y]
    checked = vbuf.at[prow]
    rows_over = [remote(own_rows, lbuf.at[z, 0], zs.at[nz], zr.at[nz], twin)]
    z1 = [remote(lbuf.at[z], lbuf.at[z], zs.at[n], zr.at[n], peer) for n, peer in enumerate(z_peers)]
    z2 = [remote(lbuf, lbuf, zs.at[nz - 1], zr.at[nz - 1], twin)]
    c1 = [remote(wp_row, wp_row, cs.at[0, n], cr.at[0, n], peer) for n, peer in enumerate(x_peers)]
    c2 = [remote(wp_column, wp_column, cs.at[1, n], cr.at[1, n], peer) for n, peer in enumerate(y_peers)]
    wp_over = [remote(wp, wp, cs.at[4, 0], cr.at[4, 0], twin)]
    c3 = [remote(sums_row, sums_row, cs.at[2, n], cr.at[2, n], peer) for n, peer in enumerate(x_peers)]
    c4 = [remote(sums_column, sums_column, cs.at[3, n], cr.at[3, n], peer) for n, peer in enumerate(y_peers)]
    c5 = [remote(checked, checked, us.at[n], ur.at[n], peer) for n, peer in enumerate(plane_peers)]
    u_over = [remote(usum, usum, cs.at[4, 1], cr.at[4, 1], twin)]

    loads[2].wait()

    @on(0)
    def _():
        pl.semaphore_wait(barrier, 13)
        begin(rows_over)

    place = jnp.where(piv[...] - base == row_ids, 1.0, 0.0)


    for n in range(NCH):
        mat_load(n).wait()
        cols = chunk_cols(n)
        block = mat[:, cols]
        high = block.astype(jnp.bfloat16)
        middle = (block - high.astype(jnp.float32)).astype(jnp.bfloat16)
        picked = bdot(picks[...], middle) + bdot(picks[...], high)
        contrib[:, cols] = jnp.where(top, block, picked[0:NB])
        q = (n % 2) * 2 + n // 2
        sums_row[pl.ds(2 * q, 2), :] = picked[NB : NB + 2] + picked[NB + 8 : NB + 10]
        if n == 0:
            @on(1)
            def _():
                landed(rows_over)

        begin(up_outer(n))

        if n == 1:
            @on(0)
            def _():
                wp_row[...] = few_rows(w8[...], (place.astype(jnp.bfloat16),))
                begin(c1)


    @on(1)
    def _():
        lbuf[z, 1] = own_rows[...]
        pl.semaphore_wait(barrier, len(line))
        begin(z1)

    holders = piv_cols >> 8
    owners[...] = holders
    owners_b[0] = holders & (SIDE - 1)
    owners_b[1] = holders >> 2
    loads[3].wait()
    linv_high[...], linv_low[...] = split(linv[...])

    for n in range(NCH):
        r = rings[n % 2]
        landed(up_outer(n))
        rows = r.rows[0]
        who = owners[rows, :]
        p1 = t1 = contrib[rows, chunk_cols(n)]
        for d in (1, 2, 3):
            got = up1[n, d - 1]
            p1 = jnp.where(who == r.who[SIDE - d], got, p1)
            t1 = jnp.where(r.a == d, got, t1)
        passing = jnp.logical_and(owners_b[r.half, rows, :] != 0, r.b == 0)
        t1s[n] = t1
        v1s[n] = jnp.where(passing, t1, p1)
        begin(inner(n))

        if n == 1:
            @on(0)
            def _():
                landed(c1)
                wp_column[...] = ((wp_x[0] + wp_x[1]) + wp_x[2]) + wp_x[3]
                begin(c2)


    @on(0)
    def _():
        landed(c2)
        wp[...] = ((wp_y[0] + wp_y[1]) + wp_y[2]) + wp_y[3]
        begin(wp_over)

    keep_col = jnp.where(top, 0.0, 1.0 - jnp.sum(place, axis=1, keepdims=True))

    for n in range(NCH):
        r = rings[n % 2]
        landed(inner(n))
        rows = r.rows[0]
        who, who_b = owners[rows, :], owners_b[r.half, rows, :]
        p3, t3 = v1s[n], t1s[n]
        for d in (1, 2, 3):
            got = up2[n, d - 1]
            p3 = jnp.where(who_b == r.inner[SIDE - d], got, p3)
            t3 = jnp.where(r.b == d, got, t3)
        for d in (1, 2, 3):
            esend[n, d - 1] = jnp.where(who == r.who[d], t3, p3)
        slots[rows, chunk_cols(n)] = jnp.where(who == prow, t3, p3)
        begin(down_outer(n))

    @on(1)
    def _():
        landed(z1)
        begin(z2)

    @on(1)
    def _():
        landed(wp_over)

    @pl.when(top)
    def _():
        for q in range(4):
            part = few_rows(wp[...], split(mat[:, pl.ds(q * W, W)]))
            sums_row[pl.ds(2 * q, 2), :] = part[0:2]

    begin(c3)

    for n in range(NCH):
        left(up_outer(n))
        left(inner(n))

    @on(0)
    def _():
        landed(z2)

    lower_high, lower_low = split(jnp.where(top, jnp.where(row_ids == lane_ids, -1.0, 0.0), lbuf[...].reshape(NB, NB)))

    @on(1)
    def _():
        checked[...] = few_rows(w8[...], (lower_high, lower_low))[0:2]
        begin(c5)

    multiplier = -(
        (bdot(lower_low, linv_high[...]) + bdot(lower_high, linv_low[...])) + bdot(lower_high, linv_high[...])
    )
    factor_high[...], factor_low[...] = split(multiplier)
    places[...] = place.astype(jnp.bfloat16)
    landed(c3)
    sums_column[...] = ((sums_x[0] + sums_x[1]) + sums_x[2]) + sums_x[3]
    begin(c4)

    for n in range(NCH):
        landed(down_outer(n))
        cols = chunk_cols(n)
        got = slots[:, cols]
        got_high, got_low = split(got)
        high, low_part = split(jnp.where(owners[...] == prow, contrib[:, cols], got))
        rows_high[:, cols] = high
        rows_low[:, cols] = low_part
        product = (bdot(factor_low[...], high) + bdot(factor_high[...], low_part)) + bdot(factor_high[...], high)
        landing = bdot(places[...], got_low) + bdot(places[...], got_high)
        out_ref[:, cols] = (mat[:, cols] * keep_col + landing) + product

    @on(1)
    def _():
        landed(c5)
        usum[...] = jnp.sum(vbuf[...], axis=0)
        begin(u_over)
        left(z1 + z2 + c5)

    @on(0)
    def _():
        left(rows_over + c1 + c2 + wp_over)
        landed(u_over)

    left(c3)
    for n in range(NCH):
        left(down_outer(n))

    landed(c4)
    left(c4)
    totals[...] = ((sums_y[0] + sums_y[1]) + sums_y[2]) + sums_y[3]
    u = jnp.concatenate([usum[...], jnp.zeros((6, NB), jnp.float32)], axis=0)
    check_factor = -few_rows(u, (linv_high[...], linv_low[...]))
    for q in range(NCH):
        cols = pl.ds(q * W, W)
        added = few_rows(check_factor, (rows_high[:, cols], rows_low[:, cols]))
        chk_ref[:, cols] = added[0:2] + totals[pl.ds(2 * q, 2), :]

    @on(1)
    def _():
        left(u_over)


def hand_over(updated, checks, updated_out, checks_out, sems):
    size = NB // COPIES
    parts = [pl.ds(k * size, size) for k in range(COPIES)]
    copies = [pltpu.make_async_copy(updated.at[p], updated_out.at[p], sems.at[k]) for k, p in enumerate(parts)]
    copies.append(pltpu.make_async_copy(checks, checks_out, sems.at[COPIES]))
    for copy in copies:
        copy.start()
    for copy in copies:
        copy.wait()


def shards(nz, matrix, lpanel, linv, pivots, weights):
    f32 = jnp.float32
    columns = matrix.shape[1]
    n = NCH
    anywhere = pl.BlockSpec(memory_space=pl.ANY)
    vmem = pltpu.VMEM
    dma = pltpu.SemaphoreType.DMA
    operands = (matrix, lpanel, linv, pivots.reshape(1, NB), weights)
    updated, checks = pl.pallas_call(
        functools.partial(kernel, nz),
        out_shape=(vmem((NB, columns), f32), vmem((2, columns), f32)),
        in_specs=[anywhere] * 5,
        out_specs=(pl.BlockSpec(memory_space=vmem), pl.BlockSpec(memory_space=vmem)),
        scratch_shapes=[
            vmem((NB, columns), f32),
            vmem((NB, columns), f32),
            vmem((NB, NB), jnp.int32),
            vmem((2, NB, NB), jnp.int32),
            vmem((NB, NB), f32),
            vmem((1, NB), jnp.int32),
            vmem((8, NB), f32),
            vmem((8, NB), f32),
            vmem((nz, 2, 8, NB), f32),
            vmem((SIDE * SIDE, 2, NB), f32),
            vmem((2, NB), f32),
            vmem((n, 3, QUARTER, W), f32),
            vmem((n, QUARTER, W), f32),
            vmem((n, QUARTER, W), f32),
            vmem((n, 3, QUARTER, W), f32),
            vmem((n, 3, QUARTER, W), f32),
            vmem((NB, columns), f32),
            vmem((NB, NB), jnp.bfloat16),
            vmem((NB, NB), jnp.bfloat16),
            vmem((NB + 16, NB), jnp.bfloat16),
            vmem((NB, NB), jnp.bfloat16),
            vmem((NB, NB), jnp.bfloat16),
            vmem((NB, NB), jnp.bfloat16),
            vmem((NB, columns), jnp.bfloat16),
            vmem((NB, columns), jnp.bfloat16),
            vmem((5, 8, NB), f32),
            vmem((4, 8, NB), f32),
            vmem((4, 8, W), f32),
            vmem((4, 8, W), f32),
            vmem((8, W), f32),
            dma((4,)),
            dma((n,)),
            dma((n, 3)), dma((n, 3)), dma((n, 3)), dma((n, 3)), dma((n, 3)), dma((n, 3)),
            dma((nz + 1,)), dma((nz + 1,)), dma((SIDE * SIDE - 1,)), dma((SIDE * SIDE - 1,)),
            dma((5, 3)), dma((5, 3)),
        ],
        compiler_params=pltpu.CompilerParams(
            collective_id=0, has_side_effects=True, vmem_limit_bytes=40 * 1024 * 1024
        ),
        cost_estimate=pl.CostEstimate(flops=500_000_000, bytes_accessed=4_000_000, transcendentals=0),
    )(*[pltpu.with_memory_space_constraint(v, pltpu.HBM) for v in operands])
    return pl.pallas_call(
        hand_over,
        out_shape=(
            jax.ShapeDtypeStruct((NB, columns), f32),
            jax.ShapeDtypeStruct((2, columns), f32),
        ),
        in_specs=[anywhere] * 2,
        out_specs=(anywhere, anywhere),
        scratch_shapes=[dma((COPIES + 1,))],
        cost_estimate=pl.CostEstimate(flops=0, bytes_accessed=2_000_000, transcendentals=0),
    )(*[pltpu.with_memory_space_constraint(v, vmem) for v in (updated, checks)])


def solution(mesh):
    return jax.shard_map(
        functools.partial(shards, mesh.shape["pcol"] // 2),
        mesh=mesh,
        in_specs=(P("prow", "pcol"), P(("prow", "pcol"), None), P(), P(), P(None, "prow")),
        out_specs=(P("prow", "pcol"), P(None, "pcol")),
        check_vma=False,
    )
```

```python
import functools
import types

import jax
import jax.numpy as jnp
from jax import lax
from jax.experimental import pallas as pl
from jax.experimental.pallas import tpu as pltpu
from jax.sharding import PartitionSpec as P

MESH = pl.DeviceIdType.MESH
HIGHEST = lax.Precision.HIGHEST
NB = 256
SIDE = 4
W = 256
NCH = 4
COPIES = 8
PAIRS = ((0, 1), (2, 3))
QUARTER = NB // SIDE


def dot(a, b):
    return jnp.dot(a, b, precision=HIGHEST, preferred_element_type=jnp.float32)


def bdot(a, b):
    return jnp.dot(a, b, preferred_element_type=jnp.float32)


def split(value):
    high = value.astype(jnp.bfloat16)
    return high, (value - high.astype(jnp.float32)).astype(jnp.bfloat16)


def few_rows(rows, wide):
    pair = jnp.concatenate([piece.astype(jnp.float32) for piece in split(rows)], axis=0).astype(jnp.bfloat16)
    product = sum(bdot(pair, piece) for piece in reversed(wide))
    return product[0:8] + product[8:16]


def rows_of(start, size):
    return pl.ds(pl.multiple_of(start, size), size)


def kernel(
    nz,
    m_hbm, l_hbm, linv_hbm, piv_hbm, w_hbm,
    out_ref, chk_ref,
    mat, contrib, owners, owners_b, linv, piv, w8, own_rows, lbuf, vbuf, usum,
    up1, t1s, v1s, up2, esend, slots,
    linv_high, linv_low, picks, places, factor_high, factor_low, rows_high, rows_low, given, gathered, totals,
    load_sem, mat_sem,
    su, ru, s2, r2, sd, rd,
    zs, zr, us, ur, ts, tr,
):
    prow, pcol = lax.axis_index("prow"), lax.axis_index("pcol")
    x, y = prow // SIDE, prow % SIDE
    z, core = pcol // 2, pcol % 2
    top = prow == 0

    x_peers = [(lax.rem(x + d, SIDE) * SIDE + y, pcol) for d in (1, 2, 3)]
    y_peers = [(x * SIDE + lax.rem(y + d, SIDE), pcol) for d in (1, 2, 3)]
    far_first = sorted(range(1, nz), key=lambda d: -min(d, nz - d))
    line = [lax.rem(z + d, nz) * 2 for d in far_first]
    z_peers = [(prow, column + 1) for column in line]
    plane_peers = [(lax.rem(prow + d, SIDE * SIDE), pcol) for d in range(1, SIDE * SIDE)]
    twin = (prow, z * 2 + 1 - core)

    w8[...] = jnp.zeros_like(w8)
    loads = [
        pltpu.make_async_copy(piv_hbm, piv, load_sem.at[0]),
        pltpu.make_async_copy(w_hbm, w8.at[pl.ds(0, 2)], load_sem.at[1]),
        pltpu.make_async_copy(l_hbm, own_rows, load_sem.at[2]),
        pltpu.make_async_copy(linv_hbm, linv, load_sem.at[3]),
    ]
    for copy in loads[:2]:
        copy.start()

    def chunk_cols(n):
        return pl.ds(pl.multiple_of((n % 2) * 2 * W + (n // 2) * W, W), W)

    def mat_load(n):
        cols = chunk_cols(n)
        return pltpu.make_async_copy(m_hbm.at[:, cols], mat.at[:, cols], mat_sem.at[n])

    for n in range(NCH):
        mat_load(n).start()
    for copy in loads[2:]:
        copy.start()

    barrier = pltpu.get_barrier_semaphore()

    def greet(peer):
        pl.semaphore_signal(barrier, inc=1, device_id=peer, device_id_type=MESH)

    for row, _ in x_peers + y_peers:
        greet((row, z * 2))

    @pl.when(core == 1)
    def _():
        greet(twin)
        for column in line:
            greet((prow, column + 1))

    def remote(src, dst, send_sem, recv_sem, peer):
        return pltpu.make_async_remote_copy(
            src_ref=src, dst_ref=dst, send_sem=send_sem, recv_sem=recv_sem,
            device_id=peer, device_id_type=MESH,
        )

    def begin(copies):
        for copy in copies:
            copy.start()

    def left(copies):
        for copy in copies:
            copy.wait_send()

    def landed(copies):
        for copy in copies:
            copy.wait_recv()

    def on(which):
        return pl.when(core == which)

    loads[0].wait()
    loads[1].wait()
    base = prow * NB
    row_ids = lax.broadcasted_iota(jnp.int32, (NB, NB), 0)
    lane_ids = lax.broadcasted_iota(jnp.int32, (NB, NB), 1)
    piv_cols = jnp.transpose(jnp.broadcast_to(piv[...], (NB, NB)))
    pick = jnp.where(piv_cols - base == lane_ids, 1.0, 0.0)
    picks[pl.ds(0, NB), :] = pick.astype(jnp.bfloat16)
    keep_row = 1.0 - jnp.sum(pick, axis=0, keepdims=True)
    kept = jnp.concatenate([piece.astype(jnp.float32) for piece in split(w8[...] * keep_row)], axis=0)
    picks[pl.ds(NB, 16), :] = kept.astype(jnp.bfloat16)

    def ring_of(half):
        a, b = (x, y) if half == 0 else (y, x)

        def place(a, b):
            return a * SIDE + b if half == 0 else b * SIDE + a

        outer = {d: lax.rem(a + d, SIDE) for d in (0, 1, 2, 3)}
        inner = {d: lax.rem(b + d, SIDE) for d in (1, 2, 3)}
        return types.SimpleNamespace(
            half=half, a=a, b=b, outer=outer, inner=inner,
            who={d: place(outer[d], b) for d in outer},
            to={d: (place(outer[d], b), pcol) for d in outer},
            to_inner={d: (place(a, inner[d]), pcol) for d in inner},
            rows={d: rows_of(outer[d] * QUARTER, QUARTER) for d in outer},
        )

    rings = ring_of(0), ring_of(1)

    def up_outer(n):
        r = rings[n % 2]
        return [
            remote(
                contrib.at[r.rows[d], chunk_cols(n)], up1.at[n, d - 1], su.at[n, d - 1], ru.at[n, d - 1], r.to[d])
            for d in (1, 2, 3)
        ]

    def inner(n):
        r = rings[n % 2]
        return [
            remote(
                v1s.at[n], up2.at[n, d - 1], s2.at[n, d - 1], r2.at[n, d - 1], r.to_inner[d])
            for d in (1, 2, 3)
        ]

    def down_outer(n):
        r = rings[n % 2]
        return [
            remote(
                esend.at[n, d - 1], slots.at[r.rows[0], chunk_cols(n)], sd.at[n, d - 1], rd.at[n, d - 1], r.to[d])
            for d in (1, 2, 3)
        ]

    checked = vbuf.at[prow]
    rows_over = [remote(own_rows, lbuf.at[z, 0], zs.at[nz], zr.at[nz], twin)]
    z1 = [remote(lbuf.at[z], lbuf.at[z], zs.at[n], zr.at[n], peer) for n, peer in enumerate(z_peers)]
    z2 = [remote(lbuf, lbuf, zs.at[nz - 1], zr.at[nz - 1], twin)]
    to_top = [remote(given, gathered.at[prow], ts.at[0], tr.at[lax.rem(prow + 15, 16)], (0, pcol))]
    at_top = [remote(given, gathered.at[k], ts.at[0], tr.at[k - 1], (0, pcol)) for k in range(1, SIDE * SIDE)]
    from_top = [remote(totals, totals, ts.at[k], tr.at[SIDE * SIDE - 1], (k, pcol)) for k in range(1, SIDE * SIDE)]
    c5 = [remote(checked, checked, us.at[n], ur.at[n], peer) for n, peer in enumerate(plane_peers)]
    u_over = [remote(usum, usum, ts.at[SIDE * SIDE], tr.at[SIDE * SIDE], twin)]

    loads[2].wait()

    @on(0)
    def _():
        pl.semaphore_wait(barrier, 13)
        begin(rows_over)

    place = jnp.where(piv[...] - base == row_ids, 1.0, 0.0)


    for pair in PAIRS:
        for n in pair:
            mat_load(n).wait()
        for n in pair:
            cols = chunk_cols(n)
            block = mat[:, cols]
            high, middle = split(block)
            picked = bdot(picks[...], middle) + bdot(picks[...], high)
            contrib[:, cols] = jnp.where(top, block, picked[0:NB])
            q = (n % 2) * 2 + n // 2
            given[pl.ds(2 * q, 2), :] = picked[NB : NB + 2] + picked[NB + 8 : NB + 10]
        if pair == PAIRS[0]:
            @on(1)
            def _():
                landed(rows_over)

        for n in pair:
            begin(up_outer(n))

    @on(1)
    def _():
        lbuf[z, 1] = own_rows[...]
        pl.semaphore_wait(barrier, len(line))
        begin(z1)

    holders = piv_cols >> 8
    owners[...] = holders
    owners_b[0] = holders & (SIDE - 1)
    owners_b[1] = holders >> 2
    loads[3].wait()
    linv_high[...], linv_low[...] = split(linv[...])

    for n in range(NCH):
        r = rings[n % 2]
        landed(up_outer(n))
        rows = r.rows[0]
        who = owners[rows, :]
        p1 = t1 = contrib[rows, chunk_cols(n)]
        for d in (1, 2, 3):
            got = up1[n, d - 1]
            p1 = jnp.where(who == r.who[SIDE - d], got, p1)
            t1 = jnp.where(r.a == d, got, t1)
        passing = jnp.logical_and(owners_b[r.half, rows, :] != 0, r.b == 0)
        t1s[n] = t1
        v1s[n] = jnp.where(passing, t1, p1)
        begin(inner(n))

    @pl.when(prow != 0)
    def _():
        given[pl.ds(8, 8), :] = few_rows(w8[...], (place.astype(jnp.bfloat16),))
        begin(to_top)

    keep_col = jnp.where(top, 0.0, 1.0 - jnp.sum(place, axis=1, keepdims=True))

    for n in range(NCH):
        r = rings[n % 2]
        landed(inner(n))
        rows = r.rows[0]
        who, who_b = owners[rows, :], owners_b[r.half, rows, :]
        p3, t3 = v1s[n], t1s[n]
        for d in (1, 2, 3):
            got = up2[n, d - 1]
            p3 = jnp.where(who_b == r.inner[SIDE - d], got, p3)
            t3 = jnp.where(r.b == d, got, t3)
        for d in (1, 2, 3):
            esend[n, d - 1] = jnp.where(who == r.who[d], t3, p3)
        slots[rows, chunk_cols(n)] = jnp.where(who == prow, t3, p3)
        begin(down_outer(n))

    @on(1)
    def _():
        landed(z1)
        begin(z2)

    @pl.when(top)
    def _():
        landed(at_top)
        added = jnp.sum(gathered[1:], axis=0)
        totals[...] = added[0:8]
        part = few_rows(added[8:16], split(mat[...]))
        for q in range(NCH):
            totals[pl.ds(2 * q, 2), :] = totals[pl.ds(2 * q, 2), :] + part[0:2, q * W : (q + 1) * W]
        begin(from_top)

    for n in range(NCH):
        left(up_outer(n))
        left(inner(n))

    @on(0)
    def _():
        landed(z2)

    lower_high, lower_low = split(jnp.where(top, jnp.where(row_ids == lane_ids, -1.0, 0.0), lbuf[...].reshape(NB, NB)))

    @on(1)
    def _():
        checked[...] = few_rows(w8[...], (lower_high, lower_low))[0:2]
        begin(c5)

    multiplier = -(
        (bdot(lower_low, linv_high[...]) + bdot(lower_high, linv_low[...])) + bdot(lower_high, linv_high[...])
    )
    factor_high[...], factor_low[...] = split(multiplier)
    places[...] = place.astype(jnp.bfloat16)

    for pair in PAIRS:
        for n in pair:
            landed(down_outer(n))
        for n in pair:
            cols = chunk_cols(n)
            got = slots[:, cols]
            got_high, got_low = split(got)
            high, low_part = split(jnp.where(owners[...] == prow, contrib[:, cols], got))
            rows_high[:, cols] = high
            rows_low[:, cols] = low_part
            product = (bdot(factor_low[...], high) + bdot(factor_high[...], low_part)) + bdot(factor_high[...], high)
            landing = bdot(places[...], got_low) + bdot(places[...], got_high)
            out_ref[:, cols] = (mat[:, cols] * keep_col + landing) + product
        if pair == PAIRS[0]:
            @on(1)
            def _():
                landed(c5)
                usum[...] = jnp.sum(vbuf[...], axis=0)
                begin(u_over)

    for n in range(NCH):
        left(down_outer(n))

    @on(1)
    def _():
        left(z1 + z2 + c5)

    @on(0)
    def _():
        left(rows_over)
        landed(u_over)

    u = jnp.concatenate([usum[...], jnp.zeros((6, NB), jnp.float32)], axis=0)
    check_factor = -few_rows(u, (linv_high[...], linv_low[...]))

    @pl.when(prow != 0)
    def _():
        landed(from_top[:1])
        left(to_top)

    @pl.when(top)
    def _():
        left(from_top)

    checked_rows = few_rows(check_factor, (rows_high[...], rows_low[...]))
    for q in range(NCH):
        cols = pl.ds(q * W, W)
        chk_ref[:, cols] = checked_rows[0:2, q * W : (q + 1) * W] + totals[pl.ds(2 * q, 2), :]

    @on(1)
    def _():
        left(u_over)


def hand_over(updated, checks, updated_out, checks_out, sems):
    size = NB // COPIES
    parts = [pl.ds(k * size, size) for k in range(COPIES)]
    copies = [pltpu.make_async_copy(updated.at[p], updated_out.at[p], sems.at[k]) for k, p in enumerate(parts)]
    copies.append(pltpu.make_async_copy(checks, checks_out, sems.at[COPIES]))
    for copy in copies:
        copy.start()
    for copy in copies:
        copy.wait()


def shards(nz, matrix, lpanel, linv, pivots, weights):
    f32 = jnp.float32
    columns = matrix.shape[1]
    n = NCH
    anywhere = pl.BlockSpec(memory_space=pl.ANY)
    vmem = pltpu.VMEM
    dma = pltpu.SemaphoreType.DMA
    operands = (matrix, lpanel, linv, pivots.reshape(1, NB), weights)
    updated, checks = pl.pallas_call(
        functools.partial(kernel, nz),
        out_shape=(vmem((NB, columns), f32), vmem((2, columns), f32)),
        in_specs=[anywhere] * 5,
        out_specs=(pl.BlockSpec(memory_space=vmem), pl.BlockSpec(memory_space=vmem)),
        scratch_shapes=[
            vmem((NB, columns), f32),
            vmem((NB, columns), f32),
            vmem((NB, NB), jnp.int32),
            vmem((2, NB, NB), jnp.int32),
            vmem((NB, NB), f32),
            vmem((1, NB), jnp.int32),
            vmem((8, NB), f32),
            vmem((8, NB), f32),
            vmem((nz, 2, 8, NB), f32),
            vmem((SIDE * SIDE, 2, NB), f32),
            vmem((2, NB), f32),
            vmem((n, 3, QUARTER, W), f32),
            vmem((n, QUARTER, W), f32),
            vmem((n, QUARTER, W), f32),
            vmem((n, 3, QUARTER, W), f32),
            vmem((n, 3, QUARTER, W), f32),
            vmem((NB, columns), f32),
            vmem((NB, NB), jnp.bfloat16),
            vmem((NB, NB), jnp.bfloat16),
            vmem((NB + 16, NB), jnp.bfloat16),
            vmem((NB, NB), jnp.bfloat16),
            vmem((NB, NB), jnp.bfloat16),
            vmem((NB, NB), jnp.bfloat16),
            vmem((NB, columns), jnp.bfloat16),
            vmem((NB, columns), jnp.bfloat16),
            vmem((16, W), f32),
            vmem((SIDE * SIDE, 16, W), f32),
            vmem((8, W), f32),
            dma((4,)),
            dma((n,)),
            dma((n, 3)), dma((n, 3)), dma((n, 3)), dma((n, 3)), dma((n, 3)), dma((n, 3)),
            dma((nz + 1,)), dma((nz + 1,)), dma((SIDE * SIDE - 1,)), dma((SIDE * SIDE - 1,)),
            dma((SIDE * SIDE + 1,)), dma((SIDE * SIDE + 1,)),
        ],
        compiler_params=pltpu.CompilerParams(
            collective_id=0, has_side_effects=True, vmem_limit_bytes=40 * 1024 * 1024
        ),
        cost_estimate=pl.CostEstimate(flops=500_000_000, bytes_accessed=4_000_000, transcendentals=0),
    )(*[pltpu.with_memory_space_constraint(v, pltpu.HBM) for v in operands])
    return pl.pallas_call(
        hand_over,
        out_shape=(
            jax.ShapeDtypeStruct((NB, columns), f32),
            jax.ShapeDtypeStruct((2, columns), f32),
        ),
        in_specs=[anywhere] * 2,
        out_specs=(anywhere, anywhere),
        scratch_shapes=[dma((COPIES + 1,))],
        cost_estimate=pl.CostEstimate(flops=0, bytes_accessed=2_000_000, transcendentals=0),
    )(*[pltpu.with_memory_space_constraint(v, vmem) for v in (updated, checks)])


def solution(mesh):
    return jax.shard_map(
        functools.partial(shards, mesh.shape["pcol"] // 2),
        mesh=mesh,
        in_specs=(P("prow", "pcol"), P(("prow", "pcol"), None), P(), P(), P(None, "prow")),
        out_specs=(P("prow", "pcol"), P(None, "pcol")),
        check_vma=False,
    )
```

```python
import functools
import types

import jax
import jax.numpy as jnp
from jax import lax
from jax.experimental import pallas as pl
from jax.experimental.pallas import tpu as pltpu
from jax.sharding import PartitionSpec as P

MESH = pl.DeviceIdType.MESH
HIGHEST = lax.Precision.HIGHEST
NB = 256
SIDE = 4
W = 256
NCH = 4
COPIES = 8
PAIRS = ((0, 1), (2, 3))
QUARTER = NB // SIDE


def dot(a, b):
    return jnp.dot(a, b, precision=HIGHEST, preferred_element_type=jnp.float32)


def bdot(a, b):
    return jnp.dot(a, b, preferred_element_type=jnp.float32)


def split(value):
    high = value.astype(jnp.bfloat16)
    return high, (value - high.astype(jnp.float32)).astype(jnp.bfloat16)


def few_rows(rows, wide):
    pair = jnp.concatenate([piece.astype(jnp.float32) for piece in split(rows)], axis=0).astype(jnp.bfloat16)
    product = sum(bdot(pair, piece) for piece in reversed(wide))
    return product[0:8] + product[8:16]


def rows_of(start, size):
    return pl.ds(pl.multiple_of(start, size), size)


def kernel(
    nz,
    m_hbm, l_hbm, linv_hbm, piv_hbm, w_hbm,
    out_ref, chk_ref,
    mat, contrib, owners, owners_b, linv, piv, w8, own_rows, lbuf, vbuf,
    up1, t1s, v1s, up2, esend, slots,
    linv_high, linv_low, picks, places, factor_high, factor_low, rows_high, rows_low, given, gathered, sums, totals,
    load_sem, mat_sem,
    ru, r2, rd, ss, rs,
):
    prow, pcol = lax.axis_index("prow"), lax.axis_index("pcol")
    x, y = prow // SIDE, prow % SIDE
    z, core = pcol // 2, pcol % 2
    top = prow == 0

    x_peers = [(lax.rem(x + d, SIDE) * SIDE + y, pcol) for d in (1, 2, 3)]
    y_peers = [(x * SIDE + lax.rem(y + d, SIDE), pcol) for d in (1, 2, 3)]
    far_first = sorted(range(1, nz), key=lambda d: -min(d, nz - d))
    line = [lax.rem(z + d, nz) * 2 for d in far_first]
    z_peers = [(prow, column + 1) for column in line]
    plane_peers = [(lax.rem(prow + d, SIDE * SIDE), pcol) for d in range(1, SIDE * SIDE)]
    twin = (prow, z * 2 + 1 - core)

    w8[...] = jnp.zeros_like(w8)
    loads = [
        pltpu.make_async_copy(piv_hbm, piv, load_sem.at[0]),
        pltpu.make_async_copy(w_hbm, w8.at[pl.ds(0, 2)], load_sem.at[1]),
        pltpu.make_async_copy(l_hbm, own_rows, load_sem.at[2]),
        pltpu.make_async_copy(linv_hbm, linv, load_sem.at[3]),
    ]
    for copy in loads[:2]:
        copy.start()

    def chunk_cols(n):
        return pl.ds(pl.multiple_of((n % 2) * 2 * W + (n // 2) * W, W), W)

    def mat_load(n):
        cols = chunk_cols(n)
        return pltpu.make_async_copy(m_hbm.at[:, cols], mat.at[:, cols], mat_sem.at[n])

    for n in range(NCH):
        mat_load(n).start()
    for copy in loads[2:]:
        copy.start()

    barrier = pltpu.get_barrier_semaphore()

    def greet(peer):
        pl.semaphore_signal(barrier, inc=1, device_id=peer, device_id_type=MESH)

    for row, _ in x_peers + y_peers:
        greet((row, z * 2))

    @pl.when(core == 1)
    def _():
        greet(twin)
        for column in line:
            greet((prow, column + 1))

    def remote(src, dst, send_sem, recv_sem, peer):
        return pltpu.make_async_remote_copy(
            src_ref=src, dst_ref=dst, send_sem=send_sem, recv_sem=recv_sem,
            device_id=peer, device_id_type=MESH,
        )

    def begin(copies):
        for copy in copies:
            copy.start()

    def done(ref, sem):
        pltpu.make_async_copy(ref, ref, sem).wait()

    def on(which):
        return pl.when(core == which)

    loads[0].wait()
    loads[1].wait()
    base = prow * NB
    row_ids = lax.broadcasted_iota(jnp.int32, (NB, NB), 0)
    lane_ids = lax.broadcasted_iota(jnp.int32, (NB, NB), 1)
    piv_cols = jnp.transpose(jnp.broadcast_to(piv[...], (NB, NB)))
    pick = jnp.where(piv_cols - base == lane_ids, 1.0, 0.0)
    picks[pl.ds(0, NB), :] = pick.astype(jnp.bfloat16)
    keep_row = 1.0 - jnp.sum(pick, axis=0, keepdims=True)
    kept = jnp.concatenate([piece.astype(jnp.float32) for piece in split(w8[...] * keep_row)], axis=0)
    picks[pl.ds(NB, 16), :] = kept.astype(jnp.bfloat16)

    def ring_of(half):
        a, b = (x, y) if half == 0 else (y, x)

        def place(a, b):
            return a * SIDE + b if half == 0 else b * SIDE + a

        outer = {d: lax.rem(a + d, SIDE) for d in (0, 1, 2, 3)}
        inner = {d: lax.rem(b + d, SIDE) for d in (1, 2, 3)}
        return types.SimpleNamespace(
            half=half, a=a, b=b, outer=outer, inner=inner,
            who={d: place(outer[d], b) for d in outer},
            to={d: (place(outer[d], b), pcol) for d in outer},
            to_inner={d: (place(a, inner[d]), pcol) for d in inner},
            rows={d: rows_of(outer[d] * QUARTER, QUARTER) for d in outer},
        )

    rings = ring_of(0), ring_of(1)

    def up_outer(n):
        r = rings[n % 2]
        return [
            remote(
                contrib.at[r.rows[d], chunk_cols(n)], up1.at[n, d - 1], ss.at[0], ru.at[n], r.to[d])
            for d in (1, 2, 3)
        ]

    def inner(n):
        r = rings[n % 2]
        return [
            remote(
                v1s.at[n], up2.at[n, d - 1], ss.at[1], r2.at[n], r.to_inner[d])
            for d in (1, 2, 3)
        ]

    def down_outer(n):
        r = rings[n % 2]
        return [
            remote(
                esend.at[n, d - 1], slots.at[r.rows[0], chunk_cols(n)], ss.at[2], rd.at[n], r.to[d])
            for d in (1, 2, 3)
        ]

    checked, kept_here = vbuf.at[prow], sums.at[prow]
    rows_over = [remote(own_rows, lbuf.at[z, 0], ss.at[3], rs.at[3], twin)]
    z1 = [remote(lbuf.at[z], lbuf.at[z], ss.at[4], rs.at[4], peer) for peer in z_peers]
    z2 = [remote(lbuf, lbuf, ss.at[5], rs.at[5], twin)]
    to_top = [remote(given, gathered.at[prow], ss.at[6], rs.at[6], (0, pcol))]
    shared = [remote(kept_here, kept_here, ss.at[7], rs.at[7], peer) for peer in plane_peers]
    c5 = [remote(checked, checked, ss.at[8], rs.at[8], peer) for peer in plane_peers]

    loads[2].wait()

    @on(0)
    def _():
        pl.semaphore_wait(barrier, 13)
        begin(rows_over)

    place = jnp.where(piv[...] - base == row_ids, 1.0, 0.0)


    for pair in PAIRS:
        for n in pair:
            mat_load(n).wait()
        for n in pair:
            cols = chunk_cols(n)
            block = mat[:, cols]
            high, middle = split(block)
            picked = bdot(picks[...], middle) + bdot(picks[...], high)
            contrib[:, cols] = jnp.where(top, block, picked[0:NB])
            q = (n % 2) * 2 + n // 2
            kept_here[pl.ds(2 * q, 2), :] = picked[NB : NB + 2] + picked[NB + 8 : NB + 10]
        if pair == PAIRS[0]:
            @on(1)
            def _():
                done(own_rows, rs.at[3])

        for n in pair:
            begin(up_outer(n))

    @on(1)
    def _():
        lbuf[z, 1] = own_rows[...]
        pl.semaphore_wait(barrier, len(line))
        begin(z1)

    holders = piv_cols >> 8
    owners[...] = holders
    owners_b[0] = holders & (SIDE - 1)
    owners_b[1] = holders >> 2
    loads[3].wait()
    linv_high[...], linv_low[...] = split(linv[...])

    for n in range(NCH):
        r = rings[n % 2]
        done(up1.at[n], ru.at[n])
        rows = r.rows[0]
        who = owners[rows, :]
        p1 = t1 = contrib[rows, chunk_cols(n)]
        for d in (1, 2, 3):
            got = up1[n, d - 1]
            p1 = jnp.where(who == r.who[SIDE - d], got, p1)
            t1 = jnp.where(r.a == d, got, t1)
        passing = jnp.logical_and(owners_b[r.half, rows, :] != 0, r.b == 0)
        t1s[n] = t1
        v1s[n] = jnp.where(passing, t1, p1)
        begin(inner(n))

    @pl.when(prow != 0)
    def _():
        given[...] = few_rows(w8[...], (place.astype(jnp.bfloat16),))
        begin(to_top)

    keep_col = jnp.where(top, 0.0, 1.0 - jnp.sum(place, axis=1, keepdims=True))

    for n in range(NCH):
        r = rings[n % 2]
        done(up2.at[n], r2.at[n])
        rows = r.rows[0]
        who, who_b = owners[rows, :], owners_b[r.half, rows, :]
        p3, t3 = v1s[n], t1s[n]
        for d in (1, 2, 3):
            got = up2[n, d - 1]
            p3 = jnp.where(who_b == r.inner[SIDE - d], got, p3)
            t3 = jnp.where(r.b == d, got, t3)
        for d in (1, 2, 3):
            esend[n, d - 1] = jnp.where(who == r.who[d], t3, p3)
        slots[rows, chunk_cols(n)] = jnp.where(who == prow, t3, p3)
        begin(down_outer(n))

    @pl.when(top)
    def _():
        done(gathered.at[1:], rs.at[6])
        part = few_rows(jnp.sum(gathered[1:], axis=0), split(mat[...]))
        for q in range(NCH):
            kept_here[pl.ds(2 * q, 2), :] = part[0:2, q * W : (q + 1) * W]

    begin(shared)

    @on(1)
    def _():
        done(lbuf.at[1:], rs.at[4])
        begin(z2)

    @on(0)
    def _():
        done(lbuf, rs.at[5])

    lower_high, lower_low = split(jnp.where(top, jnp.where(row_ids == lane_ids, -1.0, 0.0), lbuf[...].reshape(NB, NB)))

    checked[...] = few_rows(w8[...], (lower_high, lower_low))[0:2]
    begin(c5)
    multiplier = -(
        (bdot(lower_low, linv_high[...]) + bdot(lower_high, linv_low[...])) + bdot(lower_high, linv_high[...])
    )
    factor_high[...], factor_low[...] = split(multiplier)
    places[...] = place.astype(jnp.bfloat16)

    for pair in PAIRS:
        for n in pair:
            done(esend.at[n], rd.at[n])
        for n in pair:
            cols = chunk_cols(n)
            got = slots[:, cols]
            got_high, got_low = split(got)
            high, low_part = split(jnp.where(owners[...] == prow, contrib[:, cols], got))
            rows_high[:, cols] = high
            rows_low[:, cols] = low_part
            product = (bdot(factor_low[...], high) + bdot(factor_high[...], low_part)) + bdot(factor_high[...], high)
            landing = bdot(places[...], got_low) + bdot(places[...], got_high)
            out_ref[:, cols] = (mat[:, cols] * keep_col + landing) + product

    done(vbuf.at[1:], rs.at[8])
    u = jnp.concatenate([jnp.sum(vbuf[...], axis=0), jnp.zeros((6, NB), jnp.float32)], axis=0)
    check_factor = -few_rows(u, (linv_high[...], linv_low[...]))

    done(sums.at[1:], rs.at[7])
    totals[...] = jnp.sum(sums[...], axis=0)
    checked_rows = few_rows(check_factor, (rows_high[...], rows_low[...]))
    for q in range(NCH):
        cols = pl.ds(q * W, W)
        chk_ref[:, cols] = checked_rows[0:2, q * W : (q + 1) * W] + totals[pl.ds(2 * q, 2), :]

    done(up1, ss.at[0])
    done(up2, ss.at[1])
    done(esend, ss.at[2])
    done(sums.at[1:], ss.at[7])
    done(vbuf.at[1:], ss.at[8])

    @on(0)
    def _():
        done(own_rows, ss.at[3])

    @on(1)
    def _():
        done(lbuf.at[1:], ss.at[4])
        done(lbuf, ss.at[5])

    @pl.when(prow != 0)
    def _():
        done(given, ss.at[6])


def hand_over(updated, checks, updated_out, checks_out, sems):
    size = NB // COPIES
    parts = [pl.ds(k * size, size) for k in range(COPIES)]
    copies = [pltpu.make_async_copy(updated.at[p], updated_out.at[p], sems.at[k]) for k, p in enumerate(parts)]
    copies.append(pltpu.make_async_copy(checks, checks_out, sems.at[COPIES]))
    for copy in copies:
        copy.start()
    for copy in copies:
        copy.wait()


def shards(nz, matrix, lpanel, linv, pivots, weights):
    f32 = jnp.float32
    columns = matrix.shape[1]
    n = NCH
    anywhere = pl.BlockSpec(memory_space=pl.ANY)
    vmem = pltpu.VMEM
    dma = pltpu.SemaphoreType.DMA
    operands = (matrix, lpanel, linv, pivots.reshape(1, NB), weights)
    updated, checks = pl.pallas_call(
        functools.partial(kernel, nz),
        out_shape=(vmem((NB, columns), f32), vmem((2, columns), f32)),
        in_specs=[anywhere] * 5,
        out_specs=(pl.BlockSpec(memory_space=vmem), pl.BlockSpec(memory_space=vmem)),
        scratch_shapes=[
            vmem((NB, columns), f32),
            vmem((NB, columns), f32),
            vmem((NB, NB), jnp.int32),
            vmem((2, NB, NB), jnp.int32),
            vmem((NB, NB), f32),
            vmem((1, NB), jnp.int32),
            vmem((8, NB), f32),
            vmem((8, NB), f32),
            vmem((nz, 2, 8, NB), f32),
            vmem((SIDE * SIDE, 2, NB), f32),
            vmem((n, 3, QUARTER, W), f32),
            vmem((n, QUARTER, W), f32),
            vmem((n, QUARTER, W), f32),
            vmem((n, 3, QUARTER, W), f32),
            vmem((n, 3, QUARTER, W), f32),
            vmem((NB, columns), f32),
            vmem((NB, NB), jnp.bfloat16),
            vmem((NB, NB), jnp.bfloat16),
            vmem((NB + 16, NB), jnp.bfloat16),
            vmem((NB, NB), jnp.bfloat16),
            vmem((NB, NB), jnp.bfloat16),
            vmem((NB, NB), jnp.bfloat16),
            vmem((NB, columns), jnp.bfloat16),
            vmem((NB, columns), jnp.bfloat16),
            vmem((8, NB), f32),
            vmem((SIDE * SIDE, 8, NB), f32),
            vmem((SIDE * SIDE, 8, W), f32),
            vmem((8, W), f32),
            dma((4,)),
            dma((n,)),
            dma((n,)), dma((n,)), dma((n,)),
            dma((9,)), dma((9,)),
        ],
        compiler_params=pltpu.CompilerParams(
            collective_id=0, has_side_effects=True, vmem_limit_bytes=40 * 1024 * 1024
        ),
        cost_estimate=pl.CostEstimate(flops=500_000_000, bytes_accessed=4_000_000, transcendentals=0),
    )(*[pltpu.with_memory_space_constraint(v, pltpu.HBM) for v in operands])
    return pl.pallas_call(
        hand_over,
        out_shape=(
            jax.ShapeDtypeStruct((NB, columns), f32),
            jax.ShapeDtypeStruct((2, columns), f32),
        ),
        in_specs=[anywhere] * 2,
        out_specs=(anywhere, anywhere),
        scratch_shapes=[dma((COPIES + 1,))],
        cost_estimate=pl.CostEstimate(flops=0, bytes_accessed=2_000_000, transcendentals=0),
    )(*[pltpu.with_memory_space_constraint(v, vmem) for v in (updated, checks)])


def solution(mesh):
    return jax.shard_map(
        functools.partial(shards, mesh.shape["pcol"] // 2),
        mesh=mesh,
        in_specs=(P("prow", "pcol"), P(("prow", "pcol"), None), P(), P(), P(None, "prow")),
        out_specs=(P("prow", "pcol"), P(None, "pcol")),
        check_vma=False,
    )
```

```python
import functools
import types

import jax
import jax.numpy as jnp
from jax import lax
from jax.experimental import pallas as pl
from jax.experimental.pallas import tpu as pltpu
from jax.sharding import PartitionSpec as P

MESH = pl.DeviceIdType.MESH
HIGHEST = lax.Precision.HIGHEST
NB = 256
SIDE = 4
W = 256
NCH = 4
COPIES = 2
PAIRS = ((0, 1), (2, 3))
QUARTER = NB // SIDE


def dot(a, b):
    return jnp.dot(a, b, precision=HIGHEST, preferred_element_type=jnp.float32)


def bdot(a, b):
    return jnp.dot(a, b, preferred_element_type=jnp.float32)


def split(value):
    high = value.astype(jnp.bfloat16)
    return high, (value - high.astype(jnp.float32)).astype(jnp.bfloat16)


def few_rows(rows, wide):
    pair = jnp.concatenate([piece.astype(jnp.float32) for piece in split(rows)], axis=0).astype(jnp.bfloat16)
    product = sum(bdot(pair, piece) for piece in reversed(wide))
    return product[0:8] + product[8:16]


def rows_of(start, size):
    return pl.ds(pl.multiple_of(start, size), size)


def kernel(
    nz,
    m_hbm, l_hbm, linv_hbm, piv_hbm, w_hbm,
    out_ref, chk_ref,
    mat, contrib, owners, owners_b, linv, piv, w8, own_rows, lbuf, vbuf,
    up1, t1s, v1s, up2, esend, slots,
    linv_high, linv_low, picks, places, factor_high, factor_low, rows_high, rows_low, given, gathered, sums, totals,
    load_sem, mat_sem,
    ru, r2, rd, ss, rs,
):
    prow, pcol = lax.axis_index("prow"), lax.axis_index("pcol")
    x, y = prow // SIDE, prow % SIDE
    z, core = pcol // 2, pcol % 2
    top = prow == 0

    x_peers = [(lax.rem(x + d, SIDE) * SIDE + y, pcol) for d in (1, 2, 3)]
    y_peers = [(x * SIDE + lax.rem(y + d, SIDE), pcol) for d in (1, 2, 3)]
    far_first = sorted(range(1, nz), key=lambda d: -min(d, nz - d))
    line = [lax.rem(z + d, nz) * 2 for d in far_first]
    z_peers = [(prow, column + 1) for column in line]
    plane_peers = [(lax.rem(prow + d, SIDE * SIDE), pcol) for d in range(1, SIDE * SIDE)]
    twin = (prow, z * 2 + 1 - core)

    w8[...] = jnp.zeros_like(w8)
    loads = [
        pltpu.make_async_copy(piv_hbm, piv, load_sem.at[0]),
        pltpu.make_async_copy(w_hbm, w8.at[pl.ds(0, 2)], load_sem.at[1]),
        pltpu.make_async_copy(l_hbm, own_rows, load_sem.at[2]),
        pltpu.make_async_copy(linv_hbm, linv, load_sem.at[3]),
    ]
    for copy in loads[:2]:
        copy.start()

    def chunk_cols(n):
        return pl.ds(pl.multiple_of((n % 2) * 2 * W + (n // 2) * W, W), W)

    def mat_load(n):
        cols = chunk_cols(n)
        return pltpu.make_async_copy(m_hbm.at[:, cols], mat.at[:, cols], mat_sem.at[n])

    for n in PAIRS[0]:
        mat_load(n).start()

    barrier = pltpu.get_barrier_semaphore()

    def greet(peer):
        pl.semaphore_signal(barrier, inc=1, device_id=peer, device_id_type=MESH)

    @pl.when(core == 1)
    def _():
        for column in line:
            greet((prow, column + 1))
        greet(twin)

    for row, _ in x_peers + y_peers:
        greet((row, z * 2))
    for copy in loads[2:]:
        copy.start()
    for n in PAIRS[1]:
        mat_load(n).start()

    def remote(src, dst, send_sem, recv_sem, peer):
        return pltpu.make_async_remote_copy(
            src_ref=src, dst_ref=dst, send_sem=send_sem, recv_sem=recv_sem,
            device_id=peer, device_id_type=MESH,
        )

    def begin(copies):
        for copy in copies:
            copy.start()

    def done(ref, sem):
        pltpu.make_async_copy(ref, ref, sem).wait()

    def on(which):
        return pl.when(core == which)

    loads[0].wait()
    loads[1].wait()
    base = prow * NB
    row_ids = lax.broadcasted_iota(jnp.int32, (NB, NB), 0)
    lane_ids = lax.broadcasted_iota(jnp.int32, (NB, NB), 1)
    piv_cols = jnp.transpose(jnp.broadcast_to(piv[...], (NB, NB)))
    pick = jnp.where(piv_cols - base == lane_ids, 1.0, 0.0)
    picks[pl.ds(0, NB), :] = pick.astype(jnp.bfloat16)
    keep_row = 1.0 - jnp.sum(pick, axis=0, keepdims=True)
    kept = jnp.concatenate([piece.astype(jnp.float32) for piece in split(w8[...] * keep_row)], axis=0)
    picks[pl.ds(NB, 16), :] = kept.astype(jnp.bfloat16)

    def ring_of(half):
        a, b = (x, y) if half == 0 else (y, x)

        def place(a, b):
            return a * SIDE + b if half == 0 else b * SIDE + a

        outer = {d: lax.rem(a + d, SIDE) for d in (0, 1, 2, 3)}
        inner = {d: lax.rem(b + d, SIDE) for d in (1, 2, 3)}
        return types.SimpleNamespace(
            half=half, a=a, b=b, outer=outer, inner=inner,
            who={d: place(outer[d], b) for d in outer},
            to={d: (place(outer[d], b), pcol) for d in outer},
            to_inner={d: (place(a, inner[d]), pcol) for d in inner},
            rows={d: rows_of(outer[d] * QUARTER, QUARTER) for d in outer},
        )

    rings = ring_of(0), ring_of(1)

    def up_outer(n):
        r = rings[n % 2]
        return [
            remote(
                contrib.at[r.rows[d], chunk_cols(n)], up1.at[n, d - 1], ss.at[0], ru.at[n], r.to[d])
            for d in (1, 2, 3)
        ]

    def inner(n):
        r = rings[n % 2]
        return [
            remote(
                v1s.at[n], up2.at[n, d - 1], ss.at[1], r2.at[n], r.to_inner[d])
            for d in (1, 2, 3)
        ]

    def down_outer(n):
        r = rings[n % 2]
        return [
            remote(
                esend.at[n, d - 1], slots.at[r.rows[0], chunk_cols(n)], ss.at[2], rd.at[n], r.to[d])
            for d in (1, 2, 3)
        ]

    checked, kept_here = vbuf.at[prow], sums.at[prow]
    rows_over = [remote(own_rows, lbuf.at[z, 0], ss.at[3], rs.at[3], twin)]
    z1 = [remote(lbuf.at[z], lbuf.at[z], ss.at[4], rs.at[4], peer) for peer in z_peers]
    z2 = [remote(lbuf, lbuf, ss.at[5], rs.at[5], twin)]
    to_top = [remote(given, gathered.at[prow], ss.at[6], rs.at[6], (0, pcol))]
    shared = [remote(kept_here, kept_here, ss.at[7], rs.at[7], peer) for peer in plane_peers]
    c5 = [remote(checked, checked, ss.at[8], rs.at[8], peer) for peer in plane_peers]

    loads[2].wait()

    @on(0)
    def _():
        pl.semaphore_wait(barrier, 13)
        begin(rows_over)

    place = jnp.where(piv[...] - base == row_ids, 1.0, 0.0)


    for pair in PAIRS:
        for n in pair:
            mat_load(n).wait()
        for n in pair:
            cols = chunk_cols(n)
            block = mat[:, cols]
            high, middle = split(block)
            picked = bdot(picks[...], middle) + bdot(picks[...], high)
            contrib[:, cols] = jnp.where(top, block, picked[0:NB])
            q = (n % 2) * 2 + n // 2
            kept_here[pl.ds(2 * q, 2), :] = picked[NB : NB + 2] + picked[NB + 8 : NB + 10]

        @on(0)
        def _():
            for n in pair:
                begin(up_outer(n))

    holders = piv_cols >> 8
    owners[...] = holders
    owners_b[0] = holders & (SIDE - 1)
    owners_b[1] = holders >> 2
    loads[3].wait()
    linv_high[...], linv_low[...] = split(linv[...])

    @on(1)
    def _():
        lbuf[z, 1] = own_rows[...]
        done(own_rows, rs.at[3])
        for n in range(NCH):
            begin(up_outer(n))
        pl.semaphore_wait(barrier, len(line))
        begin(z1)

    for n in range(NCH):
        r = rings[n % 2]
        done(up1.at[n], ru.at[n])
        rows = r.rows[0]
        who = owners[rows, :]
        p1 = t1 = contrib[rows, chunk_cols(n)]
        for d in (1, 2, 3):
            got = up1[n, d - 1]
            p1 = jnp.where(who == r.who[SIDE - d], got, p1)
            t1 = jnp.where(r.a == d, got, t1)
        passing = jnp.logical_and(owners_b[r.half, rows, :] != 0, r.b == 0)
        t1s[n] = t1
        v1s[n] = jnp.where(passing, t1, p1)
        begin(inner(n))

    @pl.when(prow != 0)
    def _():
        given[...] = few_rows(w8[...], (place.astype(jnp.bfloat16),))
        begin(to_top)

    keep_col = jnp.where(top, 0.0, 1.0 - jnp.sum(place, axis=1, keepdims=True))

    for n in range(NCH):
        r = rings[n % 2]
        done(up2.at[n], r2.at[n])
        rows = r.rows[0]
        who, who_b = owners[rows, :], owners_b[r.half, rows, :]
        p3, t3 = v1s[n], t1s[n]
        for d in (1, 2, 3):
            got = up2[n, d - 1]
            p3 = jnp.where(who_b == r.inner[SIDE - d], got, p3)
            t3 = jnp.where(r.b == d, got, t3)
        for d in (1, 2, 3):
            esend[n, d - 1] = jnp.where(who == r.who[d], t3, p3)
        slots[rows, chunk_cols(n)] = jnp.where(who == prow, t3, p3)
        begin(down_outer(n))

    @pl.when(top)
    def _():
        done(gathered.at[1:], rs.at[6])
        part = few_rows(jnp.sum(gathered[1:], axis=0), split(mat[...]))
        for q in range(NCH):
            kept_here[pl.ds(2 * q, 2), :] = part[0:2, q * W : (q + 1) * W]

    begin(shared)

    @on(1)
    def _():
        done(lbuf.at[1:], rs.at[4])
        begin(z2)

    @on(0)
    def _():
        done(lbuf, rs.at[5])

    lower_high, lower_low = split(jnp.where(top, jnp.where(row_ids == lane_ids, -1.0, 0.0), lbuf[...].reshape(NB, NB)))

    checked[...] = few_rows(w8[...], (lower_high, lower_low))[0:2]
    begin(c5)
    multiplier = -(
        (bdot(lower_low, linv_high[...]) + bdot(lower_high, linv_low[...])) + bdot(lower_high, linv_high[...])
    )
    factor_high[...], factor_low[...] = split(multiplier)
    places[...] = place.astype(jnp.bfloat16)

    for pair in PAIRS:
        for n in pair:
            done(esend.at[n], rd.at[n])
        for n in pair:
            cols = chunk_cols(n)
            got = slots[:, cols]
            got_high, got_low = split(got)
            high, low_part = split(jnp.where(owners[...] == prow, contrib[:, cols], got))
            rows_high[:, cols] = high
            rows_low[:, cols] = low_part
            product = (bdot(factor_low[...], high) + bdot(factor_high[...], low_part)) + bdot(factor_high[...], high)
            landing = bdot(places[...], got_low) + bdot(places[...], got_high)
            out_ref[:, cols] = (mat[:, cols] * keep_col + landing) + product

    done(vbuf.at[1:], rs.at[8])
    u = jnp.concatenate([jnp.sum(vbuf[...], axis=0), jnp.zeros((6, NB), jnp.float32)], axis=0)
    check_factor = -few_rows(u, (linv_high[...], linv_low[...]))

    done(sums.at[1:], rs.at[7])
    totals[...] = jnp.sum(sums[...], axis=0)
    checked_rows = few_rows(check_factor, (rows_high[...], rows_low[...]))
    for q in range(NCH):
        cols = pl.ds(q * W, W)
        chk_ref[:, cols] = checked_rows[0:2, q * W : (q + 1) * W] + totals[pl.ds(2 * q, 2), :]

    done(up1, ss.at[0])
    done(up2, ss.at[1])
    done(esend, ss.at[2])
    done(sums.at[1:], ss.at[7])
    done(vbuf.at[1:], ss.at[8])

    @on(0)
    def _():
        done(own_rows, ss.at[3])

    @on(1)
    def _():
        done(lbuf.at[1:], ss.at[4])
        done(lbuf, ss.at[5])

    @pl.when(prow != 0)
    def _():
        done(given, ss.at[6])


def hand_over(updated, checks, updated_out, checks_out, sems):
    size = NB // COPIES
    parts = [pl.ds(k * size, size) for k in range(COPIES)]
    copies = [pltpu.make_async_copy(updated.at[p], updated_out.at[p], sems.at[k]) for k, p in enumerate(parts)]
    copies.append(pltpu.make_async_copy(checks, checks_out, sems.at[COPIES]))
    for copy in copies:
        copy.start()
    for copy in copies:
        copy.wait()


def shards(nz, matrix, lpanel, linv, pivots, weights):
    f32 = jnp.float32
    columns = matrix.shape[1]
    n = NCH
    anywhere = pl.BlockSpec(memory_space=pl.ANY)
    vmem = pltpu.VMEM
    dma = pltpu.SemaphoreType.DMA
    operands = (matrix, lpanel, linv, pivots.reshape(1, NB), weights)
    updated, checks = pl.pallas_call(
        functools.partial(kernel, nz),
        out_shape=(vmem((NB, columns), f32), vmem((2, columns), f32)),
        in_specs=[anywhere] * 5,
        out_specs=(pl.BlockSpec(memory_space=vmem), pl.BlockSpec(memory_space=vmem)),
        scratch_shapes=[
            vmem((NB, columns), f32),
            vmem((NB, columns), f32),
            vmem((NB, NB), jnp.int32),
            vmem((2, NB, NB), jnp.int32),
            vmem((NB, NB), f32),
            vmem((1, NB), jnp.int32),
            vmem((8, NB), f32),
            vmem((8, NB), f32),
            vmem((nz, 2, 8, NB), f32),
            vmem((SIDE * SIDE, 2, NB), f32),
            vmem((n, 3, QUARTER, W), f32),
            vmem((n, QUARTER, W), f32),
            vmem((n, QUARTER, W), f32),
            vmem((n, 3, QUARTER, W), f32),
            vmem((n, 3, QUARTER, W), f32),
            vmem((NB, columns), f32),
            vmem((NB, NB), jnp.bfloat16),
            vmem((NB, NB), jnp.bfloat16),
            vmem((NB + 16, NB), jnp.bfloat16),
            vmem((NB, NB), jnp.bfloat16),
            vmem((NB, NB), jnp.bfloat16),
            vmem((NB, NB), jnp.bfloat16),
            vmem((NB, columns), jnp.bfloat16),
            vmem((NB, columns), jnp.bfloat16),
            vmem((8, NB), f32),
            vmem((SIDE * SIDE, 8, NB), f32),
            vmem((SIDE * SIDE, 8, W), f32),
            vmem((8, W), f32),
            dma((4,)),
            dma((n,)),
            dma((n,)), dma((n,)), dma((n,)),
            dma((9,)), dma((9,)),
        ],
        compiler_params=pltpu.CompilerParams(
            collective_id=0, has_side_effects=True, vmem_limit_bytes=40 * 1024 * 1024
        ),
        cost_estimate=pl.CostEstimate(flops=500_000_000, bytes_accessed=4_000_000, transcendentals=0),
    )(*[pltpu.with_memory_space_constraint(v, pltpu.HBM) for v in operands])
    return pl.pallas_call(
        hand_over,
        out_shape=(
            jax.ShapeDtypeStruct((NB, columns), f32),
            jax.ShapeDtypeStruct((2, columns), f32),
        ),
        in_specs=[anywhere] * 2,
        out_specs=(anywhere, anywhere),
        scratch_shapes=[dma((COPIES + 1,))],
        cost_estimate=pl.CostEstimate(flops=0, bytes_accessed=2_000_000, transcendentals=0),
    )(*[pltpu.with_memory_space_constraint(v, vmem) for v in (updated, checks)])


def solution(mesh):
    return jax.shard_map(
        functools.partial(shards, mesh.shape["pcol"] // 2),
        mesh=mesh,
        in_specs=(P("prow", "pcol"), P(("prow", "pcol"), None), P(), P(), P(None, "prow")),
        out_specs=(P("prow", "pcol"), P(None, "pcol")),
        check_vma=False,
    )
```

```python
import functools
import types

import jax
import jax.numpy as jnp
from jax import lax
from jax.experimental import pallas as pl
from jax.experimental.pallas import tpu as pltpu
from jax.sharding import PartitionSpec as P

MESH = pl.DeviceIdType.MESH
HIGHEST = lax.Precision.HIGHEST
NB = 256
SIDE = 4
W = 256
NCH = 4
COPIES = 2
PAIRS = ((0, 1), (2, 3))
QUARTER = NB // SIDE


def dot(a, b):
    return jnp.dot(a, b, precision=HIGHEST, preferred_element_type=jnp.float32)


def bdot(a, b):
    return jnp.dot(a, b, preferred_element_type=jnp.float32)


def split(value):
    high = value.astype(jnp.bfloat16)
    return high, (value - high.astype(jnp.float32)).astype(jnp.bfloat16)


def few_rows(rows, wide):
    pair = jnp.concatenate([piece.astype(jnp.float32) for piece in split(rows)], axis=0).astype(jnp.bfloat16)
    product = bdot(jnp.concatenate([pair] * len(wide), axis=1), jnp.concatenate(wide[::-1], axis=0))
    return product[0:8] + product[8:16]


def rows_of(start, size):
    return pl.ds(pl.multiple_of(start, size), size)


def kernel(
    nz,
    m_hbm, l_hbm, linv_hbm, piv_hbm, w_hbm,
    out_ref, chk_ref,
    mat, contrib, owners, owners_b, linv, piv, w8, own_rows, lbuf, vbuf,
    up1, t1s, v1s, up2, esend, slots,
    linv3, picks, factors, rows_high, rows_low, given, gathered, sums, totals,
    load_sem, mat_sem,
    ru, r2, rd, ss, rs,
):
    prow, pcol = lax.axis_index("prow"), lax.axis_index("pcol")
    x, y = prow // SIDE, prow % SIDE
    z, core = pcol // 2, pcol % 2
    top = prow == 0

    x_peers = [(lax.rem(x + d, SIDE) * SIDE + y, pcol) for d in (1, 2, 3)]
    y_peers = [(x * SIDE + lax.rem(y + d, SIDE), pcol) for d in (1, 2, 3)]
    far_first = sorted(range(1, nz), key=lambda d: -min(d, nz - d))
    line = [lax.rem(z + d, nz) * 2 for d in far_first]
    z_peers = [(prow, column + 1) for column in line]
    plane_peers = [(lax.rem(prow + d, SIDE * SIDE), pcol) for d in range(1, SIDE * SIDE)]
    twin = (prow, z * 2 + 1 - core)

    w8[...] = jnp.zeros_like(w8)
    loads = [
        pltpu.make_async_copy(piv_hbm, piv, load_sem.at[0]),
        pltpu.make_async_copy(w_hbm, w8.at[pl.ds(0, 2)], load_sem.at[1]),
        pltpu.make_async_copy(l_hbm, own_rows, load_sem.at[2]),
        pltpu.make_async_copy(linv_hbm, linv, load_sem.at[3]),
    ]
    for copy in loads[:2]:
        copy.start()

    def chunk_cols(n):
        return pl.ds(pl.multiple_of((n % 2) * 2 * W + (n // 2) * W, W), W)

    def mat_load(n):
        cols = chunk_cols(n)
        return pltpu.make_async_copy(m_hbm.at[:, cols], mat.at[:, cols], mat_sem.at[n])

    for n in PAIRS[0]:
        mat_load(n).start()

    barrier = pltpu.get_barrier_semaphore()

    def greet(peer):
        pl.semaphore_signal(barrier, inc=1, device_id=peer, device_id_type=MESH)

    @pl.when(core == 1)
    def _():
        for column in line:
            greet((prow, column + 1))
        greet(twin)

    for row, _ in x_peers + y_peers:
        greet((row, z * 2))
    for copy in loads[2:]:
        copy.start()
    for n in PAIRS[1]:
        mat_load(n).start()

    def remote(src, dst, send_sem, recv_sem, peer):
        return pltpu.make_async_remote_copy(
            src_ref=src, dst_ref=dst, send_sem=send_sem, recv_sem=recv_sem,
            device_id=peer, device_id_type=MESH,
        )

    def begin(copies):
        for copy in copies:
            copy.start()

    def done(ref, sem):
        pltpu.make_async_copy(ref, ref, sem).wait()

    def on(which):
        return pl.when(core == which)

    loads[0].wait()
    loads[1].wait()
    base = prow * NB
    row_ids = lax.broadcasted_iota(jnp.int32, (NB, NB), 0)
    lane_ids = lax.broadcasted_iota(jnp.int32, (NB, NB), 1)
    piv_cols = jnp.transpose(jnp.broadcast_to(piv[...], (NB, NB)))
    pick = jnp.where(piv_cols - base == lane_ids, 1.0, 0.0)
    picks[pl.ds(0, NB), :] = jnp.concatenate([pick.astype(jnp.bfloat16)] * 2, axis=1)
    keep_row = 1.0 - jnp.sum(pick, axis=0, keepdims=True)
    kept = jnp.concatenate([piece.astype(jnp.float32) for piece in split(w8[...] * keep_row)], axis=0)
    picks[pl.ds(NB, 16), :] = jnp.concatenate([kept.astype(jnp.bfloat16)] * 2, axis=1)

    def ring_of(half):
        a, b = (x, y) if half == 0 else (y, x)

        def place(a, b):
            return a * SIDE + b if half == 0 else b * SIDE + a

        outer = {d: lax.rem(a + d, SIDE) for d in (0, 1, 2, 3)}
        inner = {d: lax.rem(b + d, SIDE) for d in (1, 2, 3)}
        return types.SimpleNamespace(
            half=half, a=a, b=b, outer=outer, inner=inner,
            who={d: place(outer[d], b) for d in outer},
            to={d: (place(outer[d], b), pcol) for d in outer},
            to_inner={d: (place(a, inner[d]), pcol) for d in inner},
            rows={d: rows_of(outer[d] * QUARTER, QUARTER) for d in outer},
        )

    rings = ring_of(0), ring_of(1)

    def up_outer(n):
        r = rings[n % 2]
        return [
            remote(
                contrib.at[r.rows[d], chunk_cols(n)], up1.at[n, d - 1], ss.at[0], ru.at[n], r.to[d])
            for d in (1, 2, 3)
        ]

    def inner(n):
        r = rings[n % 2]
        return [
            remote(
                v1s.at[n], up2.at[n, d - 1], ss.at[1], r2.at[n], r.to_inner[d])
            for d in (1, 2, 3)
        ]

    def down_outer(n):
        r = rings[n % 2]
        return [
            remote(
                esend.at[n, d - 1], slots.at[r.rows[0], chunk_cols(n)], ss.at[2], rd.at[n], r.to[d])
            for d in (1, 2, 3)
        ]

    checked, kept_here = vbuf.at[prow], sums.at[prow]
    rows_over = [remote(own_rows, lbuf.at[z, 0], ss.at[3], rs.at[3], twin)]
    z1 = [remote(lbuf.at[z], lbuf.at[z], ss.at[4], rs.at[4], peer) for peer in z_peers]
    z2 = [remote(lbuf, lbuf, ss.at[5], rs.at[5], twin)]
    to_top = [remote(given, gathered.at[prow], ss.at[6], rs.at[6], (0, pcol))]
    shared = [remote(kept_here, kept_here, ss.at[7], rs.at[7], peer) for peer in plane_peers]
    c5 = [remote(checked, checked, ss.at[8], rs.at[8], peer) for peer in plane_peers]

    loads[2].wait()

    @on(0)
    def _():
        pl.semaphore_wait(barrier, 13)
        begin(rows_over)

    place = jnp.where(piv[...] - base == row_ids, 1.0, 0.0)


    for pair in PAIRS:
        for n in pair:
            mat_load(n).wait()
        for n in pair:
            cols = chunk_cols(n)
            block = mat[:, cols]
            high, middle = split(block)
            picked = bdot(picks[...], jnp.concatenate([middle, high], axis=0))
            contrib[:, cols] = jnp.where(top, block, picked[0:NB])
            q = (n % 2) * 2 + n // 2
            kept_here[pl.ds(2 * q, 2), :] = picked[NB : NB + 2] + picked[NB + 8 : NB + 10]

        @on(0)
        def _():
            for n in pair:
                begin(up_outer(n))

    holders = piv_cols >> 8
    owners[...] = holders
    owners_b[0] = holders & (SIDE - 1)
    owners_b[1] = holders >> 2
    loads[3].wait()
    linv_high, linv_low = split(linv[...])
    linv3[...] = jnp.concatenate([linv_high, linv_low, linv_high], axis=0)
    factors[:, pl.ds(3 * NB, 2 * NB)] = jnp.concatenate([place.astype(jnp.bfloat16)] * 2, axis=1)

    @on(1)
    def _():
        lbuf[z, 1] = own_rows[...]
        done(own_rows, rs.at[3])
        for n in range(NCH):
            begin(up_outer(n))
        pl.semaphore_wait(barrier, len(line))
        begin(z1)

    for n in range(NCH):
        r = rings[n % 2]
        done(up1.at[n], ru.at[n])
        rows = r.rows[0]
        who = owners[rows, :]
        p1 = t1 = contrib[rows, chunk_cols(n)]
        for d in (1, 2, 3):
            got = up1[n, d - 1]
            p1 = jnp.where(who == r.who[SIDE - d], got, p1)
            t1 = jnp.where(r.a == d, got, t1)
        passing = jnp.logical_and(owners_b[r.half, rows, :] != 0, r.b == 0)
        t1s[n] = t1
        v1s[n] = jnp.where(passing, t1, p1)
        begin(inner(n))

    @pl.when(prow != 0)
    def _():
        given[...] = few_rows(w8[...], (place.astype(jnp.bfloat16),))
        begin(to_top)

    keep_col = jnp.where(top, 0.0, 1.0 - jnp.sum(place, axis=1, keepdims=True))

    for n in range(NCH):
        r = rings[n % 2]
        done(up2.at[n], r2.at[n])
        rows = r.rows[0]
        who, who_b = owners[rows, :], owners_b[r.half, rows, :]
        p3, t3 = v1s[n], t1s[n]
        for d in (1, 2, 3):
            got = up2[n, d - 1]
            p3 = jnp.where(who_b == r.inner[SIDE - d], got, p3)
            t3 = jnp.where(r.b == d, got, t3)
        for d in (1, 2, 3):
            esend[n, d - 1] = jnp.where(who == r.who[d], t3, p3)
        slots[rows, chunk_cols(n)] = jnp.where(who == prow, t3, p3)
        begin(down_outer(n))

    @pl.when(top)
    def _():
        done(gathered.at[1:], rs.at[6])
        part = few_rows(jnp.sum(gathered[1:], axis=0), split(mat[...]))
        for q in range(NCH):
            kept_here[pl.ds(2 * q, 2), :] = part[0:2, q * W : (q + 1) * W]

    begin(shared)

    @on(1)
    def _():
        done(lbuf.at[1:], rs.at[4])
        begin(z2)

    @on(0)
    def _():
        done(lbuf, rs.at[5])

    lower_high, lower_low = split(jnp.where(top, jnp.where(row_ids == lane_ids, -1.0, 0.0), lbuf[...].reshape(NB, NB)))

    checked[...] = few_rows(w8[...], (lower_high, lower_low))[0:2]
    begin(c5)
    multiplier = -bdot(jnp.concatenate([lower_low, lower_high, lower_high], axis=1), linv3[...])
    high, low_part = split(multiplier)
    factors[:, pl.ds(0, 3 * NB)] = jnp.concatenate([low_part, high, high], axis=1)

    for pair in PAIRS:
        for n in pair:
            done(esend.at[n], rd.at[n])
        for n in pair:
            cols = chunk_cols(n)
            got = slots[:, cols]
            got_high, got_low = split(got)
            high, low_part = split(jnp.where(owners[...] == prow, contrib[:, cols], got))
            rows_high[:, cols] = high
            rows_low[:, cols] = low_part
            product = bdot(factors[...], jnp.concatenate([high, low_part, high, got_low, got_high], axis=0))
            out_ref[:, cols] = mat[:, cols] * keep_col + product

    done(vbuf.at[1:], rs.at[8])
    u = jnp.concatenate([jnp.sum(vbuf[...], axis=0), jnp.zeros((6, NB), jnp.float32)], axis=0)
    check_factor = -few_rows(u, (linv3[pl.ds(0, NB), :], linv3[pl.ds(NB, NB), :]))

    done(sums.at[1:], rs.at[7])
    totals[...] = jnp.sum(sums[...], axis=0)
    checked_rows = few_rows(check_factor, (rows_high[...], rows_low[...]))
    for q in range(NCH):
        cols = pl.ds(q * W, W)
        chk_ref[:, cols] = checked_rows[0:2, q * W : (q + 1) * W] + totals[pl.ds(2 * q, 2), :]

    done(up1, ss.at[0])
    done(up2, ss.at[1])
    done(esend, ss.at[2])
    done(sums.at[1:], ss.at[7])
    done(vbuf.at[1:], ss.at[8])

    @on(0)
    def _():
        done(own_rows, ss.at[3])

    @on(1)
    def _():
        done(lbuf.at[1:], ss.at[4])
        done(lbuf, ss.at[5])

    @pl.when(prow != 0)
    def _():
        done(given, ss.at[6])


def hand_over(updated, checks, updated_out, checks_out, sems):
    size = NB // COPIES
    parts = [pl.ds(k * size, size) for k in range(COPIES)]
    copies = [pltpu.make_async_copy(updated.at[p], updated_out.at[p], sems.at[k]) for k, p in enumerate(parts)]
    copies.append(pltpu.make_async_copy(checks, checks_out, sems.at[COPIES]))
    for copy in copies:
        copy.start()
    for copy in copies:
        copy.wait()


def shards(nz, matrix, lpanel, linv, pivots, weights):
    f32 = jnp.float32
    columns = matrix.shape[1]
    n = NCH
    anywhere = pl.BlockSpec(memory_space=pl.ANY)
    vmem = pltpu.VMEM
    dma = pltpu.SemaphoreType.DMA
    operands = (matrix, lpanel, linv, pivots.reshape(1, NB), weights)
    updated, checks = pl.pallas_call(
        functools.partial(kernel, nz),
        out_shape=(vmem((NB, columns), f32), vmem((2, columns), f32)),
        in_specs=[anywhere] * 5,
        out_specs=(pl.BlockSpec(memory_space=vmem), pl.BlockSpec(memory_space=vmem)),
        scratch_shapes=[
            vmem((NB, columns), f32),
            vmem((NB, columns), f32),
            vmem((NB, NB), jnp.int32),
            vmem((2, NB, NB), jnp.int32),
            vmem((NB, NB), f32),
            vmem((1, NB), jnp.int32),
            vmem((8, NB), f32),
            vmem((8, NB), f32),
            vmem((nz, 2, 8, NB), f32),
            vmem((SIDE * SIDE, 2, NB), f32),
            vmem((n, 3, QUARTER, W), f32),
            vmem((n, QUARTER, W), f32),
            vmem((n, QUARTER, W), f32),
            vmem((n, 3, QUARTER, W), f32),
            vmem((n, 3, QUARTER, W), f32),
            vmem((NB, columns), f32),
            vmem((3 * NB, NB), jnp.bfloat16),
            vmem((NB + 16, 2 * NB), jnp.bfloat16),
            vmem((NB, 5 * NB), jnp.bfloat16),
            vmem((NB, columns), jnp.bfloat16),
            vmem((NB, columns), jnp.bfloat16),
            vmem((8, NB), f32),
            vmem((SIDE * SIDE, 8, NB), f32),
            vmem((SIDE * SIDE, 8, W), f32),
            vmem((8, W), f32),
            dma((4,)),
            dma((n,)),
            dma((n,)), dma((n,)), dma((n,)),
            dma((9,)), dma((9,)),
        ],
        compiler_params=pltpu.CompilerParams(
            collective_id=0, has_side_effects=True, vmem_limit_bytes=40 * 1024 * 1024
        ),
        cost_estimate=pl.CostEstimate(flops=500_000_000, bytes_accessed=4_000_000, transcendentals=0),
    )(*[pltpu.with_memory_space_constraint(v, pltpu.HBM) for v in operands])
    return pl.pallas_call(
        hand_over,
        out_shape=(
            jax.ShapeDtypeStruct((NB, columns), f32),
            jax.ShapeDtypeStruct((2, columns), f32),
        ),
        in_specs=[anywhere] * 2,
        out_specs=(anywhere, anywhere),
        scratch_shapes=[dma((COPIES + 1,))],
        cost_estimate=pl.CostEstimate(flops=0, bytes_accessed=2_000_000, transcendentals=0),
    )(*[pltpu.with_memory_space_constraint(v, vmem) for v in (updated, checks)])


def solution(mesh):
    return jax.shard_map(
        functools.partial(shards, mesh.shape["pcol"] // 2),
        mesh=mesh,
        in_specs=(P("prow", "pcol"), P(("prow", "pcol"), None), P(), P(), P(None, "prow")),
        out_specs=(P("prow", "pcol"), P(None, "pcol")),
        check_vma=False,
    )
```

```python
import functools
import types

import jax
import jax.numpy as jnp
from jax import lax
from jax.experimental import pallas as pl
from jax.experimental.pallas import tpu as pltpu
from jax.sharding import PartitionSpec as P

MESH = pl.DeviceIdType.MESH
HIGHEST = lax.Precision.HIGHEST
NB = 256
SIDE = 4
W = 256
NCH = 4
COPIES = 2
PAIRS = ((0, 1), (2, 3))
QUARTER = NB // SIDE


def dot(a, b):
    return jnp.dot(a, b, precision=HIGHEST, preferred_element_type=jnp.float32)


def bdot(a, b):
    return jnp.dot(a, b, preferred_element_type=jnp.float32)


def split(value):
    high = value.astype(jnp.bfloat16)
    return high, (value - high.astype(jnp.float32)).astype(jnp.bfloat16)


def few_rows(rows, wide):
    pair = jnp.concatenate([piece.astype(jnp.float32) for piece in split(rows)], axis=0).astype(jnp.bfloat16)
    product = bdot(jnp.concatenate([pair] * len(wide), axis=1), jnp.concatenate(wide[::-1], axis=0))
    return product[0:8] + product[8:16]


def rows_of(start, size):
    return pl.ds(pl.multiple_of(start, size), size)


def kernel(
    nz,
    m_hbm, l_hbm, linv_hbm, piv_hbm, w_hbm,
    out_ref, chk_ref,
    mat, contrib, owners, owners_b, linv, piv, w8, own_rows, lbuf, vbuf,
    up1, t1s, v1s, up2, esend, slots,
    linv3, picks, factors, rows_high, rows_low, given, gathered, sums, totals,
    load_sem, mat_sem,
    ru, r2, rd, ss, rs,
):
    prow, pcol = lax.axis_index("prow"), lax.axis_index("pcol")
    x, y = prow // SIDE, prow % SIDE
    z, core = pcol // 2, pcol % 2
    top = prow == 0

    x_peers = [(lax.rem(x + d, SIDE) * SIDE + y, pcol) for d in (1, 2, 3)]
    y_peers = [(x * SIDE + lax.rem(y + d, SIDE), pcol) for d in (1, 2, 3)]
    far_first = sorted(range(1, nz), key=lambda d: -min(d, nz - d))
    line = [lax.rem(z + d, nz) * 2 for d in far_first]
    z_peers = [(prow, column + 1) for column in line]
    plane_peers = [(lax.rem(prow + d, SIDE * SIDE), pcol) for d in range(1, SIDE * SIDE)]
    twin = (prow, z * 2 + 1 - core)

    w8[...] = jnp.zeros_like(w8)
    loads = [
        pltpu.make_async_copy(piv_hbm, piv, load_sem.at[0]),
        pltpu.make_async_copy(w_hbm, w8.at[pl.ds(0, 2)], load_sem.at[1]),
        pltpu.make_async_copy(l_hbm, own_rows, load_sem.at[2]),
        pltpu.make_async_copy(linv_hbm, linv, load_sem.at[3]),
    ]
    for copy in loads[:2]:
        copy.start()

    def chunk_cols(n):
        return pl.ds(pl.multiple_of((n % 2) * 2 * W + (n // 2) * W, W), W)

    def mat_load(n):
        cols = chunk_cols(n)
        return pltpu.make_async_copy(m_hbm.at[:, cols], mat.at[:, cols], mat_sem.at[n])

    for n in PAIRS[0]:
        mat_load(n).start()

    barrier = pltpu.get_barrier_semaphore()

    def greet(peer):
        pl.semaphore_signal(barrier, inc=1, device_id=peer, device_id_type=MESH)

    @pl.when(core == 1)
    def _():
        for column in line:
            greet((prow, column + 1))
        greet(twin)

    for row, _ in x_peers + y_peers:
        greet((row, z * 2))
    for copy in loads[2:]:
        copy.start()
    for n in PAIRS[1]:
        mat_load(n).start()

    def remote(src, dst, send_sem, recv_sem, peer):
        return pltpu.make_async_remote_copy(
            src_ref=src, dst_ref=dst, send_sem=send_sem, recv_sem=recv_sem,
            device_id=peer, device_id_type=MESH,
        )

    def begin(copies):
        for copy in copies:
            copy.start()

    def done(ref, sem):
        pltpu.make_async_copy(ref, ref, sem).wait()

    def on(which):
        return pl.when(core == which)

    loads[0].wait()
    loads[1].wait()
    base = prow * NB
    row_ids = lax.broadcasted_iota(jnp.int32, (NB, NB), 0)
    lane_ids = lax.broadcasted_iota(jnp.int32, (NB, NB), 1)
    piv_cols = jnp.transpose(jnp.broadcast_to(piv[...], (NB, NB)))
    pick = jnp.where(piv_cols - base == lane_ids, 1.0, 0.0)
    picks[pl.ds(0, NB), :] = jnp.concatenate([pick.astype(jnp.bfloat16)] * 2, axis=1)
    keep_row = 1.0 - jnp.sum(pick, axis=0, keepdims=True)
    kept = jnp.concatenate([piece.astype(jnp.float32) for piece in split(w8[...] * keep_row)], axis=0)
    picks[pl.ds(NB, 16), :] = jnp.concatenate([kept.astype(jnp.bfloat16)] * 2, axis=1)

    def ring_of(half):
        a, b = (x, y) if half == 0 else (y, x)

        def place(a, b):
            return a * SIDE + b if half == 0 else b * SIDE + a

        outer = {d: lax.rem(a + d, SIDE) for d in (0, 1, 2, 3)}
        inner = {d: lax.rem(b + d, SIDE) for d in (1, 2, 3)}
        return types.SimpleNamespace(
            half=half, a=a, b=b, outer=outer, inner=inner,
            who={d: place(outer[d], b) for d in outer},
            to={d: (place(outer[d], b), pcol) for d in outer},
            to_inner={d: (place(a, inner[d]), pcol) for d in inner},
            rows={d: rows_of(outer[d] * QUARTER, QUARTER) for d in outer},
        )

    rings = ring_of(0), ring_of(1)

    def up_outer(n):
        r = rings[n % 2]
        return [
            remote(
                contrib.at[r.rows[d], chunk_cols(n)], up1.at[n, d - 1], ss.at[0], ru.at[n], r.to[d])
            for d in (1, 2, 3)
        ]

    def inner(n):
        r = rings[n % 2]
        return [
            remote(
                v1s.at[n], up2.at[n, d - 1], ss.at[1], r2.at[n], r.to_inner[d])
            for d in (1, 2, 3)
        ]

    def down_outer(n):
        r = rings[n % 2]
        return [
            remote(
                esend.at[n, d - 1], slots.at[r.rows[0], chunk_cols(n)], ss.at[2], rd.at[n], r.to[d])
            for d in (1, 2, 3)
        ]

    checked, kept_here = vbuf.at[prow], sums.at[prow]
    rows_over = [remote(own_rows, lbuf.at[z, 0], ss.at[3], rs.at[3], twin)]
    z1 = [remote(lbuf.at[z], lbuf.at[z], ss.at[4], rs.at[4], peer) for peer in z_peers]
    z2 = [remote(lbuf, lbuf, ss.at[5], rs.at[5], twin)]
    to_top = [remote(given, gathered.at[prow], ss.at[6], rs.at[6], (0, pcol))]
    shared = [remote(kept_here, kept_here, ss.at[7], rs.at[7], peer) for peer in plane_peers]
    c5 = [remote(checked, checked, ss.at[8], rs.at[8], peer) for peer in plane_peers]

    loads[2].wait()

    @on(0)
    def _():
        pl.semaphore_wait(barrier, 13)
        begin(rows_over)

    place = jnp.where(piv[...] - base == row_ids, 1.0, 0.0)


    for pair in PAIRS:
        for n in pair:
            mat_load(n).wait()
        for n in pair:
            cols = chunk_cols(n)
            block = mat[:, cols]
            high, middle = split(block)
            picked = bdot(picks[...], jnp.concatenate([middle, high], axis=0))
            contrib[:, cols] = jnp.where(top, block, picked[0:NB])
            q = (n % 2) * 2 + n // 2
            kept_here[pl.ds(2 * q, 2), :] = picked[NB : NB + 2] + picked[NB + 8 : NB + 10]

        @on(0)
        def _():
            for n in pair:
                begin(up_outer(n))

    holders = piv_cols >> 8
    owners[...] = holders
    owners_b[0] = holders & (SIDE - 1)
    owners_b[1] = holders >> 2
    loads[3].wait()
    linv_high, linv_low = split(linv[...])
    linv3[...] = jnp.concatenate([linv_high, linv_low, linv_high], axis=0)
    factors[:, pl.ds(3 * NB, 2 * NB)] = jnp.concatenate([place.astype(jnp.bfloat16)] * 2, axis=1)

    @on(1)
    def _():
        lbuf[z, 1] = own_rows[...]
        done(own_rows, rs.at[3])
        for n in range(NCH):
            begin(up_outer(n))

    def gather_panel():
        pl.semaphore_wait(barrier, len(line))
        begin(z1)

    ahead = z < nz // 8
    pl.when(jnp.logical_and(core == 1, jnp.logical_not(ahead)))(gather_panel)

    for n in range(NCH):
        r = rings[n % 2]
        done(up1.at[n], ru.at[n])
        rows = r.rows[0]
        who = owners[rows, :]
        p1 = t1 = contrib[rows, chunk_cols(n)]
        for d in (1, 2, 3):
            got = up1[n, d - 1]
            p1 = jnp.where(who == r.who[SIDE - d], got, p1)
            t1 = jnp.where(r.a == d, got, t1)
        passing = jnp.logical_and(owners_b[r.half, rows, :] != 0, r.b == 0)
        t1s[n] = t1
        v1s[n] = jnp.where(passing, t1, p1)
        begin(inner(n))

    @pl.when(prow != 0)
    def _():
        given[...] = few_rows(w8[...], (place.astype(jnp.bfloat16),))
        begin(to_top)

    keep_col = jnp.where(top, 0.0, 1.0 - jnp.sum(place, axis=1, keepdims=True))

    for n in range(NCH):
        r = rings[n % 2]
        done(up2.at[n], r2.at[n])
        rows = r.rows[0]
        who, who_b = owners[rows, :], owners_b[r.half, rows, :]
        p3, t3 = v1s[n], t1s[n]
        for d in (1, 2, 3):
            got = up2[n, d - 1]
            p3 = jnp.where(who_b == r.inner[SIDE - d], got, p3)
            t3 = jnp.where(r.b == d, got, t3)
        for d in (1, 2, 3):
            esend[n, d - 1] = jnp.where(who == r.who[d], t3, p3)
        slots[rows, chunk_cols(n)] = jnp.where(who == prow, t3, p3)
        begin(down_outer(n))

    pl.when(jnp.logical_and(core == 1, ahead))(gather_panel)

    @pl.when(top)
    def _():
        done(gathered.at[1:], rs.at[6])
        part = few_rows(jnp.sum(gathered[1:], axis=0), split(mat[...]))
        for q in range(NCH):
            kept_here[pl.ds(2 * q, 2), :] = part[0:2, q * W : (q + 1) * W]

    begin(shared)

    @on(1)
    def _():
        done(lbuf.at[1:], rs.at[4])
        begin(z2)

    @on(0)
    def _():
        done(lbuf, rs.at[5])

    lower_high, lower_low = split(jnp.where(top, jnp.where(row_ids == lane_ids, -1.0, 0.0), lbuf[...].reshape(NB, NB)))

    checked[...] = few_rows(w8[...], (lower_high, lower_low))[0:2]
    begin(c5)
    multiplier = -bdot(jnp.concatenate([lower_low, lower_high, lower_high], axis=1), linv3[...])
    high, low_part = split(multiplier)
    factors[:, pl.ds(0, 3 * NB)] = jnp.concatenate([low_part, high, high], axis=1)

    for pair in PAIRS:
        for n in pair:
            done(esend.at[n], rd.at[n])
        for n in pair:
            cols = chunk_cols(n)
            got = slots[:, cols]
            got_high, got_low = split(got)
            high, low_part = split(jnp.where(owners[...] == prow, contrib[:, cols], got))
            rows_high[:, cols] = high
            rows_low[:, cols] = low_part
            product = bdot(factors[...], jnp.concatenate([high, low_part, high, got_low, got_high], axis=0))
            out_ref[:, cols] = mat[:, cols] * keep_col + product

    done(vbuf.at[1:], rs.at[8])
    u = jnp.concatenate([jnp.sum(vbuf[...], axis=0), jnp.zeros((6, NB), jnp.float32)], axis=0)
    check_factor = -few_rows(u, (linv3[pl.ds(0, NB), :], linv3[pl.ds(NB, NB), :]))

    done(sums.at[1:], rs.at[7])
    totals[...] = jnp.sum(sums[...], axis=0)
    checked_rows = few_rows(check_factor, (rows_high[...], rows_low[...]))
    for q in range(NCH):
        cols = pl.ds(q * W, W)
        chk_ref[:, cols] = checked_rows[0:2, q * W : (q + 1) * W] + totals[pl.ds(2 * q, 2), :]

    done(up1, ss.at[0])
    done(up2, ss.at[1])
    done(esend, ss.at[2])
    done(sums.at[1:], ss.at[7])
    done(vbuf.at[1:], ss.at[8])

    @on(0)
    def _():
        done(own_rows, ss.at[3])

    @on(1)
    def _():
        done(lbuf.at[1:], ss.at[4])
        done(lbuf, ss.at[5])

    @pl.when(prow != 0)
    def _():
        done(given, ss.at[6])


def hand_over(updated, checks, updated_out, checks_out, sems):
    size = NB // COPIES
    parts = [pl.ds(k * size, size) for k in range(COPIES)]
    copies = [pltpu.make_async_copy(updated.at[p], updated_out.at[p], sems.at[k]) for k, p in enumerate(parts)]
    copies.append(pltpu.make_async_copy(checks, checks_out, sems.at[COPIES]))
    for copy in copies:
        copy.start()
    for copy in copies:
        copy.wait()


def shards(nz, matrix, lpanel, linv, pivots, weights):
    f32 = jnp.float32
    columns = matrix.shape[1]
    n = NCH
    anywhere = pl.BlockSpec(memory_space=pl.ANY)
    vmem = pltpu.VMEM
    dma = pltpu.SemaphoreType.DMA
    operands = (matrix, lpanel, linv, pivots.reshape(1, NB), weights)
    updated, checks = pl.pallas_call(
        functools.partial(kernel, nz),
        out_shape=(vmem((NB, columns), f32), vmem((2, columns), f32)),
        in_specs=[anywhere] * 5,
        out_specs=(pl.BlockSpec(memory_space=vmem), pl.BlockSpec(memory_space=vmem)),
        scratch_shapes=[
            vmem((NB, columns), f32),
            vmem((NB, columns), f32),
            vmem((NB, NB), jnp.int32),
            vmem((2, NB, NB), jnp.int32),
            vmem((NB, NB), f32),
            vmem((1, NB), jnp.int32),
            vmem((8, NB), f32),
            vmem((8, NB), f32),
            vmem((nz, 2, 8, NB), f32),
            vmem((SIDE * SIDE, 2, NB), f32),
            vmem((n, 3, QUARTER, W), f32),
            vmem((n, QUARTER, W), f32),
            vmem((n, QUARTER, W), f32),
            vmem((n, 3, QUARTER, W), f32),
            vmem((n, 3, QUARTER, W), f32),
            vmem((NB, columns), f32),
            vmem((3 * NB, NB), jnp.bfloat16),
            vmem((NB + 16, 2 * NB), jnp.bfloat16),
            vmem((NB, 5 * NB), jnp.bfloat16),
            vmem((NB, columns), jnp.bfloat16),
            vmem((NB, columns), jnp.bfloat16),
            vmem((8, NB), f32),
            vmem((SIDE * SIDE, 8, NB), f32),
            vmem((SIDE * SIDE, 8, W), f32),
            vmem((8, W), f32),
            dma((4,)),
            dma((n,)),
            dma((n,)), dma((n,)), dma((n,)),
            dma((9,)), dma((9,)),
        ],
        compiler_params=pltpu.CompilerParams(
            collective_id=0, has_side_effects=True, vmem_limit_bytes=40 * 1024 * 1024
        ),
        cost_estimate=pl.CostEstimate(flops=500_000_000, bytes_accessed=4_000_000, transcendentals=0),
    )(*[pltpu.with_memory_space_constraint(v, pltpu.HBM) for v in operands])
    return pl.pallas_call(
        hand_over,
        out_shape=(
            jax.ShapeDtypeStruct((NB, columns), f32),
            jax.ShapeDtypeStruct((2, columns), f32),
        ),
        in_specs=[anywhere] * 2,
        out_specs=(anywhere, anywhere),
        scratch_shapes=[dma((COPIES + 1,))],
        cost_estimate=pl.CostEstimate(flops=0, bytes_accessed=2_000_000, transcendentals=0),
    )(*[pltpu.with_memory_space_constraint(v, vmem) for v in (updated, checks)])


def solution(mesh):
    return jax.shard_map(
        functools.partial(shards, mesh.shape["pcol"] // 2),
        mesh=mesh,
        in_specs=(P("prow", "pcol"), P(("prow", "pcol"), None), P(), P(), P(None, "prow")),
        out_specs=(P("prow", "pcol"), P(None, "pcol")),
        check_vma=False,
    )
```

```python
import functools
import types

import jax
import jax.numpy as jnp
from jax import lax
from jax.experimental import pallas as pl
from jax.experimental.pallas import tpu as pltpu
from jax.sharding import PartitionSpec as P

MESH = pl.DeviceIdType.MESH
HIGHEST = lax.Precision.HIGHEST
NB = 256
SIDE = 4
W = 256
NCH = 4
COPIES = 2
PAIRS = ((0, 1), (2, 3))
QUARTER = NB // SIDE


def dot(a, b):
    return jnp.dot(a, b, precision=HIGHEST, preferred_element_type=jnp.float32)


def bdot(a, b):
    return jnp.dot(a, b, preferred_element_type=jnp.float32)


def split(value):
    high = value.astype(jnp.bfloat16)
    return high, (value - high.astype(jnp.float32)).astype(jnp.bfloat16)


def few_rows(rows, wide):
    pair = jnp.concatenate([piece.astype(jnp.float32) for piece in split(rows)], axis=0).astype(jnp.bfloat16)
    product = bdot(jnp.concatenate([pair] * len(wide), axis=1), jnp.concatenate(wide[::-1], axis=0))
    return product[0:8] + product[8:16]


def rows_of(start, size):
    return pl.ds(pl.multiple_of(start, size), size)


def kernel(
    nz,
    m_hbm, l_hbm, linv_hbm, piv_hbm, w_hbm,
    out_ref, chk_ref,
    mat, contrib, owners, owners_b, linv, piv, w8, own_rows, lbuf, vbuf,
    up1, t1s, v1s, up2, esend, slots,
    linv3, picks, factors, rows_high, rows_low, given, gathered, sums, totals,
    load_sem, mat_sem,
    ru, r2, rd, ss, rs,
):
    prow, pcol = lax.axis_index("prow"), lax.axis_index("pcol")
    x, y = prow // SIDE, prow % SIDE
    z, core = pcol // 2, pcol % 2
    top = prow == 0

    x_peers = [(lax.rem(x + d, SIDE) * SIDE + y, pcol) for d in (1, 2, 3)]
    y_peers = [(x * SIDE + lax.rem(y + d, SIDE), pcol) for d in (1, 2, 3)]
    far_first = sorted(range(1, nz), key=lambda d: -min(d, nz - d))
    line = [lax.rem(z + d, nz) * 2 for d in far_first]
    z_peers = [(prow, column) for column in line]
    plane_peers = [(lax.rem(prow + d, SIDE * SIDE), pcol) for d in range(1, SIDE * SIDE)]
    twin = (prow, z * 2 + 1 - core)

    w8[...] = jnp.zeros_like(w8)
    loads = [
        pltpu.make_async_copy(piv_hbm, piv, load_sem.at[0]),
        pltpu.make_async_copy(w_hbm, w8.at[pl.ds(0, 2)], load_sem.at[1]),
        pltpu.make_async_copy(l_hbm, own_rows, load_sem.at[2]),
        pltpu.make_async_copy(linv_hbm, linv, load_sem.at[3]),
    ]
    for copy in loads[:2]:
        copy.start()

    def chunk_cols(n):
        return pl.ds(pl.multiple_of((n % 2) * 2 * W + (n // 2) * W, W), W)

    def mat_load(n):
        cols = chunk_cols(n)
        return pltpu.make_async_copy(m_hbm.at[:, cols], mat.at[:, cols], mat_sem.at[n])

    for n in PAIRS[0]:
        mat_load(n).start()

    barrier = pltpu.get_barrier_semaphore()

    def greet(peer):
        pl.semaphore_signal(barrier, inc=1, device_id=peer, device_id_type=MESH)

    @pl.when(core == 0)
    def _():
        for column in line:
            greet((prow, column))
        greet(twin)

    for row, _ in x_peers + y_peers:
        greet((row, z * 2 + 1))
    for copy in loads[2:]:
        copy.start()
    for n in PAIRS[1]:
        mat_load(n).start()

    def remote(src, dst, send_sem, recv_sem, peer):
        return pltpu.make_async_remote_copy(
            src_ref=src, dst_ref=dst, send_sem=send_sem, recv_sem=recv_sem,
            device_id=peer, device_id_type=MESH,
        )

    def begin(copies):
        for copy in copies:
            copy.start()

    def done(ref, sem):
        pltpu.make_async_copy(ref, ref, sem).wait()

    def on(which):
        return pl.when(core == which)

    loads[0].wait()
    loads[1].wait()
    base = prow * NB
    row_ids = lax.broadcasted_iota(jnp.int32, (NB, NB), 0)
    lane_ids = lax.broadcasted_iota(jnp.int32, (NB, NB), 1)
    piv_cols = jnp.transpose(jnp.broadcast_to(piv[...], (NB, NB)))
    pick = jnp.where(piv_cols - base == lane_ids, 1.0, 0.0)
    picks[pl.ds(0, NB), :] = jnp.concatenate([pick.astype(jnp.bfloat16)] * 2, axis=1)
    keep_row = 1.0 - jnp.sum(pick, axis=0, keepdims=True)
    kept = jnp.concatenate([piece.astype(jnp.float32) for piece in split(w8[...] * keep_row)], axis=0)
    picks[pl.ds(NB, 16), :] = jnp.concatenate([kept.astype(jnp.bfloat16)] * 2, axis=1)

    def ring_of(half):
        a, b = (x, y) if half == 0 else (y, x)

        def place(a, b):
            return a * SIDE + b if half == 0 else b * SIDE + a

        outer = {d: lax.rem(a + d, SIDE) for d in (0, 1, 2, 3)}
        inner = {d: lax.rem(b + d, SIDE) for d in (1, 2, 3)}
        return types.SimpleNamespace(
            half=half, a=a, b=b, outer=outer, inner=inner,
            who={d: place(outer[d], b) for d in outer},
            to={d: (place(outer[d], b), pcol) for d in outer},
            to_inner={d: (place(a, inner[d]), pcol) for d in inner},
            rows={d: rows_of(outer[d] * QUARTER, QUARTER) for d in outer},
        )

    rings = ring_of(0), ring_of(1)

    def up_outer(n):
        r = rings[n % 2]
        return [
            remote(
                contrib.at[r.rows[d], chunk_cols(n)], up1.at[n, d - 1], ss.at[0], ru.at[n], r.to[d])
            for d in (1, 2, 3)
        ]

    def inner(n):
        r = rings[n % 2]
        return [
            remote(
                v1s.at[n], up2.at[n, d - 1], ss.at[1], r2.at[n], r.to_inner[d])
            for d in (1, 2, 3)
        ]

    def down_outer(n):
        r = rings[n % 2]
        return [
            remote(
                esend.at[n, d - 1], slots.at[r.rows[0], chunk_cols(n)], ss.at[2], rd.at[n], r.to[d])
            for d in (1, 2, 3)
        ]

    checked, kept_here = vbuf.at[prow], sums.at[prow]
    rows_over = [remote(own_rows, lbuf.at[z, 1], ss.at[3], rs.at[3], twin)]
    z1 = [remote(lbuf.at[z], lbuf.at[z], ss.at[4], rs.at[4], peer) for peer in z_peers]
    z2 = [remote(lbuf, lbuf, ss.at[5], rs.at[5], twin)]
    to_top = [remote(given, gathered.at[prow], ss.at[6], rs.at[6], (0, pcol))]
    shared = [remote(kept_here, kept_here, ss.at[7], rs.at[7], peer) for peer in plane_peers]
    c5 = [remote(checked, checked, ss.at[8], rs.at[8], peer) for peer in plane_peers]

    loads[2].wait()

    @on(1)
    def _():
        pl.semaphore_wait(barrier, 13)
        begin(rows_over)

    place = jnp.where(piv[...] - base == row_ids, 1.0, 0.0)


    for pair in PAIRS:
        for n in pair:
            mat_load(n).wait()
        for n in pair:
            cols = chunk_cols(n)
            block = mat[:, cols]
            high, middle = split(block)
            picked = bdot(picks[...], jnp.concatenate([middle, high], axis=0))
            contrib[:, cols] = jnp.where(top, block, picked[0:NB])
            q = (n % 2) * 2 + n // 2
            kept_here[pl.ds(2 * q, 2), :] = picked[NB : NB + 2] + picked[NB + 8 : NB + 10]

        @on(1)
        def _():
            for n in pair:
                begin(up_outer(n))

    holders = piv_cols >> 8
    owners[...] = holders
    owners_b[0] = holders & (SIDE - 1)
    owners_b[1] = holders >> 2
    loads[3].wait()
    linv_high, linv_low = split(linv[...])
    linv3[...] = jnp.concatenate([linv_high, linv_low, linv_high], axis=0)
    factors[:, pl.ds(3 * NB, 2 * NB)] = jnp.concatenate([place.astype(jnp.bfloat16)] * 2, axis=1)

    @on(0)
    def _():
        lbuf[z, 0] = own_rows[...]
        done(own_rows, rs.at[3])
        for n in range(NCH):
            begin(up_outer(n))
        pl.semaphore_wait(barrier, len(line))
        begin(z1)

    for n in range(NCH):
        r = rings[n % 2]
        done(up1.at[n], ru.at[n])
        rows = r.rows[0]
        who = owners[rows, :]
        p1 = t1 = contrib[rows, chunk_cols(n)]
        for d in (1, 2, 3):
            got = up1[n, d - 1]
            p1 = jnp.where(who == r.who[SIDE - d], got, p1)
            t1 = jnp.where(r.a == d, got, t1)
        passing = jnp.logical_and(owners_b[r.half, rows, :] != 0, r.b == 0)
        t1s[n] = t1
        v1s[n] = jnp.where(passing, t1, p1)
        begin(inner(n))

    @pl.when(prow != 0)
    def _():
        given[...] = few_rows(w8[...], (place.astype(jnp.bfloat16),))
        begin(to_top)

    keep_col = jnp.where(top, 0.0, 1.0 - jnp.sum(place, axis=1, keepdims=True))

    for n in range(NCH):
        r = rings[n % 2]
        done(up2.at[n], r2.at[n])
        rows = r.rows[0]
        who, who_b = owners[rows, :], owners_b[r.half, rows, :]
        p3, t3 = v1s[n], t1s[n]
        for d in (1, 2, 3):
            got = up2[n, d - 1]
            p3 = jnp.where(who_b == r.inner[SIDE - d], got, p3)
            t3 = jnp.where(r.b == d, got, t3)
        for d in (1, 2, 3):
            esend[n, d - 1] = jnp.where(who == r.who[d], t3, p3)
        slots[rows, chunk_cols(n)] = jnp.where(who == prow, t3, p3)
        begin(down_outer(n))

    @pl.when(top)
    def _():
        done(gathered.at[1:], rs.at[6])
        part = few_rows(jnp.sum(gathered[1:], axis=0), split(mat[...]))
        for q in range(NCH):
            kept_here[pl.ds(2 * q, 2), :] = part[0:2, q * W : (q + 1) * W]

    begin(shared)

    @on(0)
    def _():
        done(lbuf.at[1:], rs.at[4])
        begin(z2)

    @on(1)
    def _():
        done(lbuf, rs.at[5])

    lower_high, lower_low = split(jnp.where(top, jnp.where(row_ids == lane_ids, -1.0, 0.0), lbuf[...].reshape(NB, NB)))

    checked[...] = few_rows(w8[...], (lower_high, lower_low))[0:2]
    begin(c5)
    multiplier = -bdot(jnp.concatenate([lower_low, lower_high, lower_high], axis=1), linv3[...])
    high, low_part = split(multiplier)
    factors[:, pl.ds(0, 3 * NB)] = jnp.concatenate([low_part, high, high], axis=1)

    for pair in PAIRS:
        for n in pair:
            done(esend.at[n], rd.at[n])
        for n in pair:
            cols = chunk_cols(n)
            got = slots[:, cols]
            got_high, got_low = split(got)
            high, low_part = split(jnp.where(owners[...] == prow, contrib[:, cols], got))
            rows_high[:, cols] = high
            rows_low[:, cols] = low_part
            product = bdot(factors[...], jnp.concatenate([high, low_part, high, got_low, got_high], axis=0))
            out_ref[:, cols] = mat[:, cols] * keep_col + product

    done(vbuf.at[1:], rs.at[8])
    u = jnp.concatenate([jnp.sum(vbuf[...], axis=0), jnp.zeros((6, NB), jnp.float32)], axis=0)
    check_factor = -few_rows(u, (linv3[pl.ds(0, NB), :], linv3[pl.ds(NB, NB), :]))

    done(sums.at[1:], rs.at[7])
    totals[...] = jnp.sum(sums[...], axis=0)
    checked_rows = few_rows(check_factor, (rows_high[...], rows_low[...]))
    for q in range(NCH):
        cols = pl.ds(q * W, W)
        chk_ref[:, cols] = checked_rows[0:2, q * W : (q + 1) * W] + totals[pl.ds(2 * q, 2), :]

    done(up1, ss.at[0])
    done(up2, ss.at[1])
    done(esend, ss.at[2])
    done(sums.at[1:], ss.at[7])
    done(vbuf.at[1:], ss.at[8])

    @on(1)
    def _():
        done(own_rows, ss.at[3])

    @on(0)
    def _():
        done(lbuf.at[1:], ss.at[4])
        done(lbuf, ss.at[5])

    @pl.when(prow != 0)
    def _():
        done(given, ss.at[6])


def hand_over(updated, checks, updated_out, checks_out, sems):
    size = NB // COPIES
    parts = [pl.ds(k * size, size) for k in range(COPIES)]
    copies = [pltpu.make_async_copy(updated.at[p], updated_out.at[p], sems.at[k]) for k, p in enumerate(parts)]
    copies.append(pltpu.make_async_copy(checks, checks_out, sems.at[COPIES]))
    for copy in copies:
        copy.start()
    for copy in copies:
        copy.wait()


def shards(nz, matrix, lpanel, linv, pivots, weights):
    f32 = jnp.float32
    columns = matrix.shape[1]
    n = NCH
    anywhere = pl.BlockSpec(memory_space=pl.ANY)
    vmem = pltpu.VMEM
    dma = pltpu.SemaphoreType.DMA
    operands = (matrix, lpanel, linv, pivots.reshape(1, NB), weights)
    updated, checks = pl.pallas_call(
        functools.partial(kernel, nz),
        out_shape=(vmem((NB, columns), f32), vmem((2, columns), f32)),
        in_specs=[anywhere] * 5,
        out_specs=(pl.BlockSpec(memory_space=vmem), pl.BlockSpec(memory_space=vmem)),
        scratch_shapes=[
            vmem((NB, columns), f32),
            vmem((NB, columns), f32),
            vmem((NB, NB), jnp.int32),
            vmem((2, NB, NB), jnp.int32),
            vmem((NB, NB), f32),
            vmem((1, NB), jnp.int32),
            vmem((8, NB), f32),
            vmem((8, NB), f32),
            vmem((nz, 2, 8, NB), f32),
            vmem((SIDE * SIDE, 2, NB), f32),
            vmem((n, 3, QUARTER, W), f32),
            vmem((n, QUARTER, W), f32),
            vmem((n, QUARTER, W), f32),
            vmem((n, 3, QUARTER, W), f32),
            vmem((n, 3, QUARTER, W), f32),
            vmem((NB, columns), f32),
            vmem((3 * NB, NB), jnp.bfloat16),
            vmem((NB + 16, 2 * NB), jnp.bfloat16),
            vmem((NB, 5 * NB), jnp.bfloat16),
            vmem((NB, columns), jnp.bfloat16),
            vmem((NB, columns), jnp.bfloat16),
            vmem((8, NB), f32),
            vmem((SIDE * SIDE, 8, NB), f32),
            vmem((SIDE * SIDE, 8, W), f32),
            vmem((8, W), f32),
            dma((4,)),
            dma((n,)),
            dma((n,)), dma((n,)), dma((n,)),
            dma((9,)), dma((9,)),
        ],
        compiler_params=pltpu.CompilerParams(
            collective_id=0, has_side_effects=True, vmem_limit_bytes=40 * 1024 * 1024
        ),
        cost_estimate=pl.CostEstimate(flops=500_000_000, bytes_accessed=4_000_000, transcendentals=0),
    )(*[pltpu.with_memory_space_constraint(v, pltpu.HBM) for v in operands])
    return pl.pallas_call(
        hand_over,
        out_shape=(
            jax.ShapeDtypeStruct((NB, columns), f32),
            jax.ShapeDtypeStruct((2, columns), f32),
        ),
        in_specs=[anywhere] * 2,
        out_specs=(anywhere, anywhere),
        scratch_shapes=[dma((COPIES + 1,))],
        cost_estimate=pl.CostEstimate(flops=0, bytes_accessed=2_000_000, transcendentals=0),
    )(*[pltpu.with_memory_space_constraint(v, vmem) for v in (updated, checks)])


def solution(mesh):
    return jax.shard_map(
        functools.partial(shards, mesh.shape["pcol"] // 2),
        mesh=mesh,
        in_specs=(P("prow", "pcol"), P(("prow", "pcol"), None), P(), P(), P(None, "prow")),
        out_specs=(P("prow", "pcol"), P(None, "pcol")),
        check_vma=False,
    )
```

```python
import functools
import types

import jax
import jax.numpy as jnp
from jax import lax
from jax.experimental import pallas as pl
from jax.experimental.pallas import tpu as pltpu
from jax.sharding import PartitionSpec as P

MESH = pl.DeviceIdType.MESH
HIGHEST = lax.Precision.HIGHEST
NB = 256
SIDE = 4
W = 256
NCH = 4
COPIES = 2
PAIRS = ((0, 1), (2, 3))
QUARTER = NB // SIDE


def dot(a, b):
    return jnp.dot(a, b, precision=HIGHEST, preferred_element_type=jnp.float32)


def bdot(a, b):
    return jnp.dot(a, b, preferred_element_type=jnp.float32)


def split(value):
    high = value.astype(jnp.bfloat16)
    return high, (value - high.astype(jnp.float32)).astype(jnp.bfloat16)


def few_rows(rows, wide):
    pair = jnp.concatenate([piece.astype(jnp.float32) for piece in split(rows)], axis=0).astype(jnp.bfloat16)
    product = bdot(jnp.concatenate([pair] * len(wide), axis=1), jnp.concatenate(wide[::-1], axis=0))
    return product[0:8] + product[8:16]


def rows_of(start, size):
    return pl.ds(pl.multiple_of(start, size), size)


def kernel(
    nz,
    m_hbm, l_hbm, linv_hbm, piv_hbm, w_hbm,
    out_ref, chk_ref,
    mat, contrib, owners, owners_b, linv, piv, w8, own_rows, lbuf, vbuf,
    up1, t1s, v1s, up2, esend, slots,
    linv3, picks, factors, rows_high, rows_low, given, gathered, sums, totals,
    load_sem, mat_sem,
    ru, r2, rd, ss, rs,
):
    prow, pcol = lax.axis_index("prow"), lax.axis_index("pcol")
    x, y = prow // SIDE, prow % SIDE
    z, core = pcol // 2, pcol % 2
    top = prow == 0

    x_peers = [(lax.rem(x + d, SIDE) * SIDE + y, pcol) for d in (1, 2, 3)]
    y_peers = [(x * SIDE + lax.rem(y + d, SIDE), pcol) for d in (1, 2, 3)]
    far_first = sorted(range(1, nz), key=lambda d: -min(d, nz - d))
    line = [lax.rem(z + d, nz) * 2 for d in far_first]
    z_peers = [(prow, column) for column in line]
    plane_peers = [(lax.rem(prow + d, SIDE * SIDE), pcol) for d in range(1, SIDE * SIDE)]
    twin = (prow, z * 2 + 1 - core)

    w8[...] = jnp.zeros_like(w8)
    loads = [
        pltpu.make_async_copy(piv_hbm, piv, load_sem.at[0]),
        pltpu.make_async_copy(w_hbm, w8.at[pl.ds(0, 2)], load_sem.at[1]),
        pltpu.make_async_copy(l_hbm, own_rows, load_sem.at[2]),
        pltpu.make_async_copy(linv_hbm, linv, load_sem.at[3]),
    ]
    for copy in loads[:2]:
        copy.start()

    def chunk_cols(n):
        return pl.ds(pl.multiple_of((n % 2) * 2 * W + (n // 2) * W, W), W)

    def mat_load(n):
        cols = chunk_cols(n)
        return pltpu.make_async_copy(m_hbm.at[:, cols], mat.at[:, cols], mat_sem.at[n])

    for n in PAIRS[0]:
        mat_load(n).start()

    barrier = pltpu.get_barrier_semaphore()

    def greet(peer):
        pl.semaphore_signal(barrier, inc=1, device_id=peer, device_id_type=MESH)

    @pl.when(core == 0)
    def _():
        for column in line:
            greet((prow, column))
        greet(twin)

    for row, _ in x_peers + y_peers:
        greet((row, z * 2 + 1))
    for copy in loads[2:]:
        copy.start()
    for n in PAIRS[1]:
        mat_load(n).start()

    def remote(src, dst, send_sem, recv_sem, peer):
        return pltpu.make_async_remote_copy(
            src_ref=src, dst_ref=dst, send_sem=send_sem, recv_sem=recv_sem,
            device_id=peer, device_id_type=MESH,
        )

    def begin(copies):
        for copy in copies:
            copy.start()

    def done(ref, sem):
        pltpu.make_async_copy(ref, ref, sem).wait()

    def on(which):
        return pl.when(core == which)

    loads[0].wait()
    loads[1].wait()
    base = prow * NB
    row_ids = lax.broadcasted_iota(jnp.int32, (NB, NB), 0)
    lane_ids = lax.broadcasted_iota(jnp.int32, (NB, NB), 1)
    piv_cols = jnp.transpose(jnp.broadcast_to(piv[...], (NB, NB)))
    pick = jnp.where(piv_cols - base == lane_ids, 1.0, 0.0)
    picks[pl.ds(0, NB), :] = jnp.concatenate([pick.astype(jnp.bfloat16)] * 2, axis=1)
    keep_row = 1.0 - jnp.sum(pick, axis=0, keepdims=True)
    kept = jnp.concatenate([piece.astype(jnp.float32) for piece in split(w8[...] * keep_row)], axis=0)
    picks[pl.ds(NB, 16), :] = jnp.concatenate([kept.astype(jnp.bfloat16)] * 2, axis=1)

    def ring_of(half):
        a, b = (x, y) if half == 0 else (y, x)

        def place(a, b):
            return a * SIDE + b if half == 0 else b * SIDE + a

        outer = {d: lax.rem(a + d, SIDE) for d in (0, 1, 2, 3)}
        inner = {d: lax.rem(b + d, SIDE) for d in (1, 2, 3)}
        return types.SimpleNamespace(
            half=half, a=a, b=b, outer=outer, inner=inner,
            who={d: place(outer[d], b) for d in outer},
            to={d: (place(outer[d], b), pcol) for d in outer},
            to_inner={d: (place(a, inner[d]), pcol) for d in inner},
            rows={d: rows_of(outer[d] * QUARTER, QUARTER) for d in outer},
        )

    rings = ring_of(0), ring_of(1)

    def up_outer(n):
        r = rings[n % 2]
        return [
            remote(
                contrib.at[r.rows[d], chunk_cols(n)], up1.at[n, d - 1], ss.at[0], ru.at[n], r.to[d])
            for d in (1, 2, 3)
        ]

    def inner(n):
        r = rings[n % 2]
        return [
            remote(
                v1s.at[n], up2.at[n, d - 1], ss.at[1], r2.at[n], r.to_inner[d])
            for d in (1, 2, 3)
        ]

    def down_outer(n):
        r = rings[n % 2]
        return [
            remote(
                esend.at[n, d - 1], slots.at[r.rows[0], chunk_cols(n)], ss.at[2], rd.at[n], r.to[d])
            for d in (1, 2, 3)
        ]

    checked, kept_here = vbuf.at[prow], sums.at[prow]
    rows_over = [remote(own_rows, lbuf.at[z, 1], ss.at[3], rs.at[3], twin)]
    z1 = [remote(lbuf.at[z], lbuf.at[z], ss.at[4], rs.at[4], peer) for peer in z_peers]
    z2 = [remote(lbuf, lbuf, ss.at[5], rs.at[5], twin)]
    to_top = [remote(given, gathered.at[prow], ss.at[6], rs.at[6], (0, pcol))]
    shared = [remote(kept_here, kept_here, ss.at[7], rs.at[7], peer) for peer in plane_peers]
    c5 = [remote(checked, checked, ss.at[8], rs.at[8], peer) for peer in plane_peers]

    loads[2].wait()

    @on(1)
    def _():
        pl.semaphore_wait(barrier, 13)
        begin(rows_over)

    place = jnp.where(piv[...] - base == row_ids, 1.0, 0.0)


    for pair in PAIRS:
        for n in pair:
            mat_load(n).wait()
        for n in pair:
            cols = chunk_cols(n)
            block = mat[:, cols]
            high, middle = split(block)
            picked = bdot(picks[...], jnp.concatenate([middle, high], axis=0))
            contrib[:, cols] = jnp.where(top, block, picked[0:NB])
            q = (n % 2) * 2 + n // 2
            kept_here[pl.ds(2 * q, 2), :] = picked[NB : NB + 2] + picked[NB + 8 : NB + 10]

        @on(1)
        def _():
            for n in pair:
                begin(up_outer(n))

    holders = piv_cols >> 8
    owners[...] = holders
    owners_b[0] = holders & (SIDE - 1)
    owners_b[1] = holders >> 2
    loads[3].wait()
    linv_high, linv_low = split(linv[...])
    linv3[...] = jnp.concatenate([linv_high, linv_low, linv_high], axis=0)
    factors[:, pl.ds(3 * NB, 2 * NB)] = jnp.concatenate([place.astype(jnp.bfloat16)] * 2, axis=1)

    @on(0)
    def _():
        lbuf[z, 0] = own_rows[...]
        done(own_rows, rs.at[3])
        for n in range(NCH):
            begin(up_outer(n))
        pl.semaphore_wait(barrier, len(line))
        begin(z1)

    for n in range(NCH):
        r = rings[n % 2]
        done(up1.at[n], ru.at[n])
        rows = r.rows[0]
        who = owners[rows, :]
        p1 = t1 = contrib[rows, chunk_cols(n)]
        for d in (1, 2, 3):
            got = up1[n, d - 1]
            p1 = jnp.where(who == r.who[SIDE - d], got, p1)
            t1 = jnp.where(r.a == d, got, t1)
        passing = jnp.logical_and(owners_b[r.half, rows, :] != 0, r.b == 0)
        t1s[n] = t1
        v1s[n] = jnp.where(passing, t1, p1)
        begin(inner(n))

    @pl.when(prow != 0)
    def _():
        given[...] = few_rows(w8[...], (place.astype(jnp.bfloat16),))
        begin(to_top)

    keep_col = jnp.where(top, 0.0, 1.0 - jnp.sum(place, axis=1, keepdims=True))

    for n in range(NCH):
        r = rings[n % 2]
        done(up2.at[n], r2.at[n])
        rows = r.rows[0]
        who, who_b = owners[rows, :], owners_b[r.half, rows, :]
        p3, t3 = v1s[n], t1s[n]
        for d in (1, 2, 3):
            got = up2[n, d - 1]
            p3 = jnp.where(who_b == r.inner[SIDE - d], got, p3)
            t3 = jnp.where(r.b == d, got, t3)
        for d in (1, 2, 3):
            esend[n, d - 1] = jnp.where(who == r.who[d], t3, p3)
        slots[rows, chunk_cols(n)] = jnp.where(who == prow, t3, p3)
        begin(down_outer(n))

    @on(0)
    def _():
        done(lbuf.at[1:], rs.at[4])
        begin(z2)

    @pl.when(top)
    def _():
        done(gathered.at[1:], rs.at[6])
        part = few_rows(jnp.sum(gathered[1:], axis=0), split(mat[...]))
        for q in range(NCH):
            kept_here[pl.ds(2 * q, 2), :] = part[0:2, q * W : (q + 1) * W]

    begin(shared)

    @on(1)
    def _():
        done(lbuf, rs.at[5])

    lower_high, lower_low = split(jnp.where(top, jnp.where(row_ids == lane_ids, -1.0, 0.0), lbuf[...].reshape(NB, NB)))

    checked[...] = few_rows(w8[...], (lower_high, lower_low))[0:2]
    begin(c5)
    multiplier = -bdot(jnp.concatenate([lower_low, lower_high, lower_high], axis=1), linv3[...])
    high, low_part = split(multiplier)
    factors[:, pl.ds(0, 3 * NB)] = jnp.concatenate([low_part, high, high], axis=1)

    for pair in PAIRS:
        for n in pair:
            done(esend.at[n], rd.at[n])
        for n in pair:
            cols = chunk_cols(n)
            got = slots[:, cols]
            got_high, got_low = split(got)
            high, low_part = split(jnp.where(owners[...] == prow, contrib[:, cols], got))
            rows_high[:, cols] = high
            rows_low[:, cols] = low_part
            product = bdot(factors[...], jnp.concatenate([high, low_part, high, got_low, got_high], axis=0))
            out_ref[:, cols] = mat[:, cols] * keep_col + product

    done(vbuf.at[1:], rs.at[8])
    u = jnp.concatenate([jnp.sum(vbuf[...], axis=0), jnp.zeros((6, NB), jnp.float32)], axis=0)
    check_factor = -few_rows(u, (linv3[pl.ds(0, NB), :], linv3[pl.ds(NB, NB), :]))

    done(sums.at[1:], rs.at[7])
    totals[...] = jnp.sum(sums[...], axis=0)
    checked_rows = few_rows(check_factor, (rows_high[...], rows_low[...]))
    for q in range(NCH):
        cols = pl.ds(q * W, W)
        chk_ref[:, cols] = checked_rows[0:2, q * W : (q + 1) * W] + totals[pl.ds(2 * q, 2), :]

    done(up1, ss.at[0])
    done(up2, ss.at[1])
    done(esend, ss.at[2])
    done(sums.at[1:], ss.at[7])
    done(vbuf.at[1:], ss.at[8])

    @on(1)
    def _():
        done(own_rows, ss.at[3])

    @on(0)
    def _():
        done(lbuf.at[1:], ss.at[4])
        done(lbuf, ss.at[5])

    @pl.when(prow != 0)
    def _():
        done(given, ss.at[6])


def hand_over(updated, checks, updated_out, checks_out, sems):
    size = NB // COPIES
    parts = [pl.ds(k * size, size) for k in range(COPIES)]
    copies = [pltpu.make_async_copy(updated.at[p], updated_out.at[p], sems.at[k]) for k, p in enumerate(parts)]
    copies.append(pltpu.make_async_copy(checks, checks_out, sems.at[COPIES]))
    for copy in copies:
        copy.start()
    for copy in copies:
        copy.wait()


def shards(nz, matrix, lpanel, linv, pivots, weights):
    f32 = jnp.float32
    columns = matrix.shape[1]
    n = NCH
    anywhere = pl.BlockSpec(memory_space=pl.ANY)
    vmem = pltpu.VMEM
    dma = pltpu.SemaphoreType.DMA
    operands = (matrix, lpanel, linv, pivots.reshape(1, NB), weights)
    updated, checks = pl.pallas_call(
        functools.partial(kernel, nz),
        out_shape=(vmem((NB, columns), f32), vmem((2, columns), f32)),
        in_specs=[anywhere] * 5,
        out_specs=(pl.BlockSpec(memory_space=vmem), pl.BlockSpec(memory_space=vmem)),
        scratch_shapes=[
            vmem((NB, columns), f32),
            vmem((NB, columns), f32),
            vmem((NB, NB), jnp.int32),
            vmem((2, NB, NB), jnp.int32),
            vmem((NB, NB), f32),
            vmem((1, NB), jnp.int32),
            vmem((8, NB), f32),
            vmem((8, NB), f32),
            vmem((nz, 2, 8, NB), f32),
            vmem((SIDE * SIDE, 2, NB), f32),
            vmem((n, 3, QUARTER, W), f32),
            vmem((n, QUARTER, W), f32),
            vmem((n, QUARTER, W), f32),
            vmem((n, 3, QUARTER, W), f32),
            vmem((n, 3, QUARTER, W), f32),
            vmem((NB, columns), f32),
            vmem((3 * NB, NB), jnp.bfloat16),
            vmem((NB + 16, 2 * NB), jnp.bfloat16),
            vmem((NB, 5 * NB), jnp.bfloat16),
            vmem((NB, columns), jnp.bfloat16),
            vmem((NB, columns), jnp.bfloat16),
            vmem((8, NB), f32),
            vmem((SIDE * SIDE, 8, NB), f32),
            vmem((SIDE * SIDE, 8, W), f32),
            vmem((8, W), f32),
            dma((4,)),
            dma((n,)),
            dma((n,)), dma((n,)), dma((n,)),
            dma((9,)), dma((9,)),
        ],
        compiler_params=pltpu.CompilerParams(
            collective_id=0, has_side_effects=True, vmem_limit_bytes=40 * 1024 * 1024
        ),
        cost_estimate=pl.CostEstimate(flops=500_000_000, bytes_accessed=4_000_000, transcendentals=0),
    )(*[pltpu.with_memory_space_constraint(v, pltpu.HBM) for v in operands])
    return pl.pallas_call(
        hand_over,
        out_shape=(
            jax.ShapeDtypeStruct((NB, columns), f32),
            jax.ShapeDtypeStruct((2, columns), f32),
        ),
        in_specs=[anywhere] * 2,
        out_specs=(anywhere, anywhere),
        scratch_shapes=[dma((COPIES + 1,))],
        cost_estimate=pl.CostEstimate(flops=0, bytes_accessed=2_000_000, transcendentals=0),
    )(*[pltpu.with_memory_space_constraint(v, vmem) for v in (updated, checks)])


def solution(mesh):
    return jax.shard_map(
        functools.partial(shards, mesh.shape["pcol"] // 2),
        mesh=mesh,
        in_specs=(P("prow", "pcol"), P(("prow", "pcol"), None), P(), P(), P(None, "prow")),
        out_specs=(P("prow", "pcol"), P(None, "pcol")),
        check_vma=False,
    )
```

```python
import functools
import types

import jax
import jax.numpy as jnp
from jax import lax
from jax.experimental import pallas as pl
from jax.experimental.pallas import tpu as pltpu
from jax.sharding import PartitionSpec as P

MESH = pl.DeviceIdType.MESH
HIGHEST = lax.Precision.HIGHEST
NB = 256
SIDE = 4
W = 256
NCH = 4
COPIES = 2
PAIRS = ((0, 1), (2, 3))
QUARTER = NB // SIDE


def dot(a, b):
    return jnp.dot(a, b, precision=HIGHEST, preferred_element_type=jnp.float32)


def bdot(a, b):
    return jnp.dot(a, b, preferred_element_type=jnp.float32)


def split(value):
    high = value.astype(jnp.bfloat16)
    return high, (value - high.astype(jnp.float32)).astype(jnp.bfloat16)


def few_rows(rows, wide):
    pair = jnp.concatenate([piece.astype(jnp.float32) for piece in split(rows)], axis=0).astype(jnp.bfloat16)
    product = bdot(jnp.concatenate([pair] * len(wide), axis=1), jnp.concatenate(wide[::-1], axis=0))
    return product[0:8] + product[8:16]


def rows_of(start, size):
    return pl.ds(pl.multiple_of(start, size), size)


def kernel(
    nz,
    m_hbm, l_hbm, linv_hbm, piv_hbm, w_hbm,
    out_ref, chk_ref,
    mat, contrib, owners, owners_b, linv, piv, w8, own_rows, lbuf, vbuf,
    up1, t1s, v1s, up2, esend, slots,
    linv3, picks, factors, rows_high, rows_low, given, gathered, sums, totals,
    load_sem, mat_sem,
    ru, r2, rd, ss, rs,
):
    prow, pcol = lax.axis_index("prow"), lax.axis_index("pcol")
    x, y = prow // SIDE, prow % SIDE
    z, core = pcol // 2, pcol % 2
    top = prow == 0

    x_peers = [(lax.rem(x + d, SIDE) * SIDE + y, pcol) for d in (1, 2, 3)]
    y_peers = [(x * SIDE + lax.rem(y + d, SIDE), pcol) for d in (1, 2, 3)]
    far_first = sorted(range(1, nz), key=lambda d: -min(d, nz - d))
    line = [lax.rem(z + d, nz) * 2 for d in far_first]
    z_peers = [(prow, column) for column in line]
    plane_peers = [(lax.rem(prow + d, SIDE * SIDE), pcol) for d in range(1, SIDE * SIDE)]
    twin = (prow, z * 2 + 1 - core)

    barrier = pltpu.get_barrier_semaphore()

    def greet(peer):
        pl.semaphore_signal(barrier, inc=1, device_id=peer, device_id_type=MESH)

    for row, _ in x_peers + y_peers:
        greet((row, z * 2 + 1))

    w8[...] = jnp.zeros_like(w8)
    loads = [
        pltpu.make_async_copy(piv_hbm, piv, load_sem.at[0]),
        pltpu.make_async_copy(w_hbm, w8.at[pl.ds(0, 2)], load_sem.at[1]),
        pltpu.make_async_copy(l_hbm, own_rows, load_sem.at[2]),
        pltpu.make_async_copy(linv_hbm, linv, load_sem.at[3]),
    ]
    for copy in loads[:2]:
        copy.start()

    def chunk_cols(n):
        return pl.ds(pl.multiple_of((n % 2) * 2 * W + (n // 2) * W, W), W)

    def mat_load(n):
        cols = chunk_cols(n)
        return pltpu.make_async_copy(m_hbm.at[:, cols], mat.at[:, cols], mat_sem.at[n])

    for n in PAIRS[0]:
        mat_load(n).start()

    @pl.when(core == 0)
    def _():
        greet(twin)
        for column in line:
            greet((prow, column))

    for copy in loads[2:]:
        copy.start()
    for n in PAIRS[1]:
        mat_load(n).start()

    def remote(src, dst, send_sem, recv_sem, peer):
        return pltpu.make_async_remote_copy(
            src_ref=src, dst_ref=dst, send_sem=send_sem, recv_sem=recv_sem,
            device_id=peer, device_id_type=MESH,
        )

    def begin(copies):
        for copy in copies:
            copy.start()

    def done(ref, sem):
        pltpu.make_async_copy(ref, ref, sem).wait()

    def on(which):
        return pl.when(core == which)

    loads[0].wait()
    loads[1].wait()
    base = prow * NB
    row_ids = lax.broadcasted_iota(jnp.int32, (NB, NB), 0)
    lane_ids = lax.broadcasted_iota(jnp.int32, (NB, NB), 1)
    piv_cols = jnp.transpose(jnp.broadcast_to(piv[...], (NB, NB)))
    pick = jnp.where(piv_cols - base == lane_ids, 1.0, 0.0)
    picks[pl.ds(0, NB), :] = jnp.concatenate([pick.astype(jnp.bfloat16)] * 2, axis=1)
    keep_row = 1.0 - jnp.sum(pick, axis=0, keepdims=True)
    kept = jnp.concatenate([piece.astype(jnp.float32) for piece in split(w8[...] * keep_row)], axis=0)
    picks[pl.ds(NB, 16), :] = jnp.concatenate([kept.astype(jnp.bfloat16)] * 2, axis=1)

    def ring_of(half):
        a, b = (x, y) if half == 0 else (y, x)

        def place(a, b):
            return a * SIDE + b if half == 0 else b * SIDE + a

        outer = {d: lax.rem(a + d, SIDE) for d in (0, 1, 2, 3)}
        inner = {d: lax.rem(b + d, SIDE) for d in (1, 2, 3)}
        return types.SimpleNamespace(
            half=half, a=a, b=b, outer=outer, inner=inner,
            who={d: place(outer[d], b) for d in outer},
            to={d: (place(outer[d], b), pcol) for d in outer},
            to_inner={d: (place(a, inner[d]), pcol) for d in inner},
            rows={d: rows_of(outer[d] * QUARTER, QUARTER) for d in outer},
        )

    rings = ring_of(0), ring_of(1)

    def up_outer(n):
        r = rings[n % 2]
        return [
            remote(
                contrib.at[r.rows[d], chunk_cols(n)], up1.at[n, d - 1], ss.at[0], ru.at[n], r.to[d])
            for d in (1, 2, 3)
        ]

    def inner(n):
        r = rings[n % 2]
        return [
            remote(
                v1s.at[n], up2.at[n, d - 1], ss.at[1], r2.at[n], r.to_inner[d])
            for d in (1, 2, 3)
        ]

    def down_outer(n):
        r = rings[n % 2]
        return [
            remote(
                esend.at[n, d - 1], slots.at[r.rows[0], chunk_cols(n)], ss.at[2], rd.at[n], r.to[d])
            for d in (1, 2, 3)
        ]

    checked, kept_here = vbuf.at[prow], sums.at[prow]
    rows_over = [remote(own_rows, lbuf.at[z, 1], ss.at[3], rs.at[3], twin)]
    z1 = [remote(lbuf.at[z], lbuf.at[z], ss.at[4], rs.at[4], peer) for peer in z_peers]
    z2 = [remote(lbuf, lbuf, ss.at[5], rs.at[5], twin)]
    to_top = [remote(given, gathered.at[prow], ss.at[6], rs.at[6], (0, pcol))]
    shared = [remote(kept_here, kept_here, ss.at[7], rs.at[7], peer) for peer in plane_peers]
    c5 = [remote(checked, checked, ss.at[8], rs.at[8], peer) for peer in plane_peers]

    loads[2].wait()

    @on(1)
    def _():
        pl.semaphore_wait(barrier, 13)
        begin(rows_over)

    place = jnp.where(piv[...] - base == row_ids, 1.0, 0.0)


    for pair in PAIRS:
        for n in pair:
            mat_load(n).wait()
        for n in pair:
            cols = chunk_cols(n)
            block = mat[:, cols]
            high, middle = split(block)
            picked = bdot(picks[...], jnp.concatenate([middle, high], axis=0))
            contrib[:, cols] = jnp.where(top, block, picked[0:NB])
            q = (n % 2) * 2 + n // 2
            kept_here[pl.ds(2 * q, 2), :] = picked[NB : NB + 2] + picked[NB + 8 : NB + 10]

        @on(1)
        def _():
            for n in pair:
                begin(up_outer(n))

    holders = piv_cols >> 8
    owners[...] = holders
    owners_b[0] = holders & (SIDE - 1)
    owners_b[1] = holders >> 2
    loads[3].wait()
    linv_high, linv_low = split(linv[...])
    linv3[...] = jnp.concatenate([linv_high, linv_low, linv_high], axis=0)
    factors[:, pl.ds(3 * NB, 2 * NB)] = jnp.concatenate([place.astype(jnp.bfloat16)] * 2, axis=1)

    @on(0)
    def _():
        lbuf[z, 0] = own_rows[...]
        done(own_rows, rs.at[3])
        for n in range(NCH):
            begin(up_outer(n))
        pl.semaphore_wait(barrier, len(line))
        begin(z1)

    for n in range(NCH):
        r = rings[n % 2]
        done(up1.at[n], ru.at[n])
        rows = r.rows[0]
        who = owners[rows, :]
        p1 = t1 = contrib[rows, chunk_cols(n)]
        for d in (1, 2, 3):
            got = up1[n, d - 1]
            p1 = jnp.where(who == r.who[SIDE - d], got, p1)
            t1 = jnp.where(r.a == d, got, t1)
        passing = jnp.logical_and(owners_b[r.half, rows, :] != 0, r.b == 0)
        t1s[n] = t1
        v1s[n] = jnp.where(passing, t1, p1)
        begin(inner(n))

    @pl.when(prow != 0)
    def _():
        given[...] = few_rows(w8[...], (place.astype(jnp.bfloat16),))
        begin(to_top)

    keep_col = jnp.where(top, 0.0, 1.0 - jnp.sum(place, axis=1, keepdims=True))

    for n in range(NCH):
        r = rings[n % 2]
        done(up2.at[n], r2.at[n])
        rows = r.rows[0]
        who, who_b = owners[rows, :], owners_b[r.half, rows, :]
        p3, t3 = v1s[n], t1s[n]
        for d in (1, 2, 3):
            got = up2[n, d - 1]
            p3 = jnp.where(who_b == r.inner[SIDE - d], got, p3)
            t3 = jnp.where(r.b == d, got, t3)
        for d in (1, 2, 3):
            esend[n, d - 1] = jnp.where(who == r.who[d], t3, p3)
        slots[rows, chunk_cols(n)] = jnp.where(who == prow, t3, p3)
        begin(down_outer(n))

    @on(0)
    def _():
        done(lbuf.at[1:], rs.at[4])
        begin(z2)

    @pl.when(top)
    def _():
        done(gathered.at[1:], rs.at[6])
        part = few_rows(jnp.sum(gathered[1:], axis=0), split(mat[...]))
        for q in range(NCH):
            kept_here[pl.ds(2 * q, 2), :] = part[0:2, q * W : (q + 1) * W]

    begin(shared)

    @on(1)
    def _():
        done(lbuf, rs.at[5])

    lower_high, lower_low = split(jnp.where(top, jnp.where(row_ids == lane_ids, -1.0, 0.0), lbuf[...].reshape(NB, NB)))

    checked[...] = few_rows(w8[...], (lower_high, lower_low))[0:2]
    begin(c5)
    multiplier = -bdot(jnp.concatenate([lower_low, lower_high, lower_high], axis=1), linv3[...])
    high, low_part = split(multiplier)
    factors[:, pl.ds(0, 3 * NB)] = jnp.concatenate([low_part, high, high], axis=1)

    for pair in PAIRS:
        for n in pair:
            done(esend.at[n], rd.at[n])
        for n in pair:
            cols = chunk_cols(n)
            got = slots[:, cols]
            got_high, got_low = split(got)
            high, low_part = split(jnp.where(owners[...] == prow, contrib[:, cols], got))
            rows_high[:, cols] = high
            rows_low[:, cols] = low_part
            product = bdot(factors[...], jnp.concatenate([high, low_part, high, got_low, got_high], axis=0))
            out_ref[:, cols] = mat[:, cols] * keep_col + product

    done(vbuf.at[1:], rs.at[8])
    u = jnp.concatenate([jnp.sum(vbuf[...], axis=0), jnp.zeros((6, NB), jnp.float32)], axis=0)
    check_factor = -few_rows(u, (linv3[pl.ds(0, NB), :], linv3[pl.ds(NB, NB), :]))

    done(sums.at[1:], rs.at[7])
    totals[...] = jnp.sum(sums[...], axis=0)
    checked_rows = few_rows(check_factor, (rows_high[...], rows_low[...]))
    for q in range(NCH):
        cols = pl.ds(q * W, W)
        chk_ref[:, cols] = checked_rows[0:2, q * W : (q + 1) * W] + totals[pl.ds(2 * q, 2), :]

    done(up1, ss.at[0])
    done(up2, ss.at[1])
    done(esend, ss.at[2])
    done(sums.at[1:], ss.at[7])
    done(vbuf.at[1:], ss.at[8])

    @on(1)
    def _():
        done(own_rows, ss.at[3])

    @on(0)
    def _():
        done(lbuf.at[1:], ss.at[4])
        done(lbuf, ss.at[5])

    @pl.when(prow != 0)
    def _():
        done(given, ss.at[6])


def hand_over(updated, checks, updated_out, checks_out, sems):
    size = NB // COPIES
    parts = [pl.ds(k * size, size) for k in range(COPIES)]
    copies = [pltpu.make_async_copy(updated.at[p], updated_out.at[p], sems.at[k]) for k, p in enumerate(parts)]
    copies.append(pltpu.make_async_copy(checks, checks_out, sems.at[COPIES]))
    for copy in copies:
        copy.start()
    for copy in copies:
        copy.wait()


def shards(nz, matrix, lpanel, linv, pivots, weights):
    f32 = jnp.float32
    columns = matrix.shape[1]
    n = NCH
    anywhere = pl.BlockSpec(memory_space=pl.ANY)
    vmem = pltpu.VMEM
    dma = pltpu.SemaphoreType.DMA
    operands = (matrix, lpanel, linv, pivots.reshape(1, NB), weights)
    updated, checks = pl.pallas_call(
        functools.partial(kernel, nz),
        out_shape=(vmem((NB, columns), f32), vmem((2, columns), f32)),
        in_specs=[anywhere] * 5,
        out_specs=(pl.BlockSpec(memory_space=vmem), pl.BlockSpec(memory_space=vmem)),
        scratch_shapes=[
            vmem((NB, columns), f32),
            vmem((NB, columns), f32),
            vmem((NB, NB), jnp.int32),
            vmem((2, NB, NB), jnp.int32),
            vmem((NB, NB), f32),
            vmem((1, NB), jnp.int32),
            vmem((8, NB), f32),
            vmem((8, NB), f32),
            vmem((nz, 2, 8, NB), f32),
            vmem((SIDE * SIDE, 2, NB), f32),
            vmem((n, 3, QUARTER, W), f32),
            vmem((n, QUARTER, W), f32),
            vmem((n, QUARTER, W), f32),
            vmem((n, 3, QUARTER, W), f32),
            vmem((n, 3, QUARTER, W), f32),
            vmem((NB, columns), f32),
            vmem((3 * NB, NB), jnp.bfloat16),
            vmem((NB + 16, 2 * NB), jnp.bfloat16),
            vmem((NB, 5 * NB), jnp.bfloat16),
            vmem((NB, columns), jnp.bfloat16),
            vmem((NB, columns), jnp.bfloat16),
            vmem((8, NB), f32),
            vmem((SIDE * SIDE, 8, NB), f32),
            vmem((SIDE * SIDE, 8, W), f32),
            vmem((8, W), f32),
            dma((4,)),
            dma((n,)),
            dma((n,)), dma((n,)), dma((n,)),
            dma((9,)), dma((9,)),
        ],
        compiler_params=pltpu.CompilerParams(
            collective_id=0, has_side_effects=True, vmem_limit_bytes=40 * 1024 * 1024
        ),
        cost_estimate=pl.CostEstimate(flops=500_000_000, bytes_accessed=4_000_000, transcendentals=0),
    )(*[pltpu.with_memory_space_constraint(v, pltpu.HBM) for v in operands])
    return pl.pallas_call(
        hand_over,
        out_shape=(
            jax.ShapeDtypeStruct((NB, columns), f32),
            jax.ShapeDtypeStruct((2, columns), f32),
        ),
        in_specs=[anywhere] * 2,
        out_specs=(anywhere, anywhere),
        scratch_shapes=[dma((COPIES + 1,))],
        cost_estimate=pl.CostEstimate(flops=0, bytes_accessed=2_000_000, transcendentals=0),
    )(*[pltpu.with_memory_space_constraint(v, vmem) for v in (updated, checks)])


def solution(mesh):
    return jax.shard_map(
        functools.partial(shards, mesh.shape["pcol"] // 2),
        mesh=mesh,
        in_specs=(P("prow", "pcol"), P(("prow", "pcol"), None), P(), P(), P(None, "prow")),
        out_specs=(P("prow", "pcol"), P(None, "pcol")),
        check_vma=False,
    )
```

```python
import functools
import types

import jax
import jax.numpy as jnp
from jax import lax
from jax.experimental import pallas as pl
from jax.experimental.pallas import tpu as pltpu
from jax.sharding import PartitionSpec as P

MESH = pl.DeviceIdType.MESH
HIGHEST = lax.Precision.HIGHEST
NB = 256
SIDE = 4
W = 256
NCH = 4
COPIES = 2
PAIRS = ((0, 1), (2, 3))
QUARTER = NB // SIDE


def dot(a, b):
    return jnp.dot(a, b, precision=HIGHEST, preferred_element_type=jnp.float32)


def bdot(a, b):
    return jnp.dot(a, b, preferred_element_type=jnp.float32)


def split(value):
    high = value.astype(jnp.bfloat16)
    return high, (value - high.astype(jnp.float32)).astype(jnp.bfloat16)


def few_rows(rows, wide):
    pair = jnp.concatenate([piece.astype(jnp.float32) for piece in split(rows)], axis=0).astype(jnp.bfloat16)
    product = bdot(jnp.concatenate([pair] * len(wide), axis=1), jnp.concatenate(wide[::-1], axis=0))
    return product[0:8] + product[8:16]


def rows_of(start, size):
    return pl.ds(pl.multiple_of(start, size), size)


def kernel(
    nz,
    m_hbm, l_hbm, linv_hbm, piv_hbm, w_hbm,
    out_ref, chk_ref,
    mat, contrib, owners, owners_b, linv, piv, w8, own_rows, lbuf, vbuf,
    up1, t1s, v1s, up2, esend, slots,
    linv3, picks, factors, rows_high, rows_low, given, gathered, sums, totals,
    load_sem, mat_sem,
    ru, r2, rd, ss, rs,
):
    prow, pcol = lax.axis_index("prow"), lax.axis_index("pcol")
    x, y = prow // SIDE, prow % SIDE
    z, core = pcol // 2, pcol % 2
    top = prow == 0

    x_peers = [(lax.rem(x + d, SIDE) * SIDE + y, pcol) for d in (1, 2, 3)]
    y_peers = [(x * SIDE + lax.rem(y + d, SIDE), pcol) for d in (1, 2, 3)]
    far_first = sorted(range(1, nz), key=lambda d: -min(d, nz - d))
    line = [lax.rem(z + d, nz) * 2 for d in far_first]
    z_peers = [(prow, column) for column in line]
    plane_peers = [(lax.rem(prow + d, SIDE * SIDE), pcol) for d in range(1, SIDE * SIDE)]
    twin = (prow, z * 2 + 1 - core)

    w8[...] = jnp.zeros_like(w8)
    loads = [
        pltpu.make_async_copy(piv_hbm, piv, load_sem.at[0]),
        pltpu.make_async_copy(w_hbm, w8.at[pl.ds(0, 2)], load_sem.at[1]),
        pltpu.make_async_copy(l_hbm, own_rows, load_sem.at[2]),
        pltpu.make_async_copy(linv_hbm, linv, load_sem.at[3]),
    ]
    for copy in loads[:2]:
        copy.start()

    def chunk_cols(n):
        return pl.ds(pl.multiple_of((n % 2) * 2 * W + (n // 2) * W, W), W)

    def mat_load(n):
        cols = chunk_cols(n)
        return pltpu.make_async_copy(m_hbm.at[:, cols], mat.at[:, cols], mat_sem.at[n])

    for n in PAIRS[0]:
        mat_load(n).start()

    barrier = pltpu.get_barrier_semaphore()

    def greet(peer):
        pl.semaphore_signal(barrier, inc=1, device_id=peer, device_id_type=MESH)

    @pl.when(core == 0)
    def _():
        for column in line:
            greet((prow, column))
        greet(twin)

    for row, _ in x_peers + y_peers:
        greet((row, z * 2 + 1))
    for copy in loads[2:]:
        copy.start()
    for n in PAIRS[1]:
        mat_load(n).start()

    def remote(src, dst, send_sem, recv_sem, peer):
        return pltpu.make_async_remote_copy(
            src_ref=src, dst_ref=dst, send_sem=send_sem, recv_sem=recv_sem,
            device_id=peer, device_id_type=MESH,
        )

    def begin(copies):
        for copy in copies:
            copy.start()

    def done(ref, sem):
        pltpu.make_async_copy(ref, ref, sem).wait()

    def on(which):
        return pl.when(core == which)

    loads[0].wait()
    loads[1].wait()
    base = prow * NB
    row_ids = lax.broadcasted_iota(jnp.int32, (NB, NB), 0)
    lane_ids = lax.broadcasted_iota(jnp.int32, (NB, NB), 1)
    piv_cols = jnp.transpose(jnp.broadcast_to(piv[...], (NB, NB)))
    pick = jnp.where(piv_cols - base == lane_ids, 1.0, 0.0)
    picks[pl.ds(0, NB), :] = jnp.concatenate([pick.astype(jnp.bfloat16)] * 2, axis=1)
    keep_row = 1.0 - jnp.sum(pick, axis=0, keepdims=True)
    kept = jnp.concatenate([piece.astype(jnp.float32) for piece in split(w8[...] * keep_row)], axis=0)
    picks[pl.ds(NB, 16), :] = jnp.concatenate([kept.astype(jnp.bfloat16)] * 2, axis=1)

    def ring_of(half):
        a, b = (x, y) if half == 0 else (y, x)

        def place(a, b):
            return a * SIDE + b if half == 0 else b * SIDE + a

        outer = {d: lax.rem(a + d, SIDE) for d in (0, 1, 2, 3)}
        inner = {d: lax.rem(b + d, SIDE) for d in (1, 2, 3)}
        return types.SimpleNamespace(
            half=half, a=a, b=b, outer=outer, inner=inner,
            who={d: place(outer[d], b) for d in outer},
            to={d: (place(outer[d], b), pcol) for d in outer},
            to_inner={d: (place(a, inner[d]), pcol) for d in inner},
            rows={d: rows_of(outer[d] * QUARTER, QUARTER) for d in outer},
        )

    rings = ring_of(0), ring_of(1)

    def up_outer(n):
        r = rings[n % 2]
        return [
            remote(
                contrib.at[r.rows[d], chunk_cols(n)], up1.at[n, d - 1], ss.at[0], ru.at[n], r.to[d])
            for d in (1, 2, 3)
        ]

    def inner(n):
        r = rings[n % 2]
        return [
            remote(
                v1s.at[n], up2.at[n, d - 1], ss.at[1], r2.at[n], r.to_inner[d])
            for d in (1, 2, 3)
        ]

    def down_outer(n):
        r = rings[n % 2]
        return [
            remote(
                esend.at[n, d - 1], slots.at[r.rows[0], chunk_cols(n)], ss.at[2], rd.at[n], r.to[d])
            for d in (1, 2, 3)
        ]

    checked, kept_here = vbuf.at[prow], sums.at[prow]
    rows_over = [remote(own_rows, lbuf.at[z, 1], ss.at[3], rs.at[3], twin)]
    z1 = [remote(lbuf.at[z], lbuf.at[z], ss.at[4], rs.at[4], peer) for peer in z_peers]
    z2 = [remote(lbuf, lbuf, ss.at[5], rs.at[5], twin)]
    to_top = [remote(given, gathered.at[prow], ss.at[6], rs.at[6], (0, pcol))]
    shared = [remote(kept_here, kept_here, ss.at[7], rs.at[7], peer) for peer in plane_peers]
    c5 = [remote(checked, checked, ss.at[8], rs.at[8], peer) for peer in plane_peers]

    loads[2].wait()

    @on(1)
    def _():
        pl.semaphore_wait(barrier, 13)
        begin(rows_over)


    for pair in ((0,), (1,), (2,), (3,)):
        for n in pair:
            mat_load(n).wait()
        for n in pair:
            cols = chunk_cols(n)
            block = mat[:, cols]
            high, middle = split(block)
            picked = bdot(picks[...], jnp.concatenate([middle, high], axis=0))
            contrib[:, cols] = jnp.where(top, block, picked[0:NB])
            q = (n % 2) * 2 + n // 2
            kept_here[pl.ds(2 * q, 2), :] = picked[NB : NB + 2] + picked[NB + 8 : NB + 10]

        @on(1)
        def _():
            for n in pair:
                begin(up_outer(n))

    place = jnp.where(piv[...] - base == row_ids, 1.0, 0.0)
    holders = piv_cols >> 8
    owners[...] = holders
    owners_b[0] = holders & (SIDE - 1)
    owners_b[1] = holders >> 2
    loads[3].wait()
    linv_high, linv_low = split(linv[...])
    linv3[...] = jnp.concatenate([linv_high, linv_low, linv_high], axis=0)
    factors[:, pl.ds(3 * NB, 2 * NB)] = jnp.concatenate([place.astype(jnp.bfloat16)] * 2, axis=1)

    @on(0)
    def _():
        lbuf[z, 0] = own_rows[...]
        done(own_rows, rs.at[3])
        for n in range(NCH):
            begin(up_outer(n))
        pl.semaphore_wait(barrier, len(line))
        begin(z1)

    for n in range(NCH):
        r = rings[n % 2]
        done(up1.at[n], ru.at[n])
        rows = r.rows[0]
        who = owners[rows, :]
        p1 = t1 = contrib[rows, chunk_cols(n)]
        for d in (1, 2, 3):
            got = up1[n, d - 1]
            p1 = jnp.where(who == r.who[SIDE - d], got, p1)
            t1 = jnp.where(r.a == d, got, t1)
        passing = jnp.logical_and(owners_b[r.half, rows, :] != 0, r.b == 0)
        t1s[n] = t1
        v1s[n] = jnp.where(passing, t1, p1)
        begin(inner(n))

    @pl.when(prow != 0)
    def _():
        given[...] = few_rows(w8[...], (place.astype(jnp.bfloat16),))
        begin(to_top)

    keep_col = jnp.where(top, 0.0, 1.0 - jnp.sum(place, axis=1, keepdims=True))

    for n in range(NCH):
        r = rings[n % 2]
        done(up2.at[n], r2.at[n])
        rows = r.rows[0]
        who, who_b = owners[rows, :], owners_b[r.half, rows, :]
        p3, t3 = v1s[n], t1s[n]
        for d in (1, 2, 3):
            got = up2[n, d - 1]
            p3 = jnp.where(who_b == r.inner[SIDE - d], got, p3)
            t3 = jnp.where(r.b == d, got, t3)
        for d in (1, 2, 3):
            esend[n, d - 1] = jnp.where(who == r.who[d], t3, p3)
        slots[rows, chunk_cols(n)] = jnp.where(who == prow, t3, p3)
        begin(down_outer(n))

    @on(0)
    def _():
        done(lbuf.at[1:], rs.at[4])
        begin(z2)

    @pl.when(top)
    def _():
        done(gathered.at[1:], rs.at[6])
        part = few_rows(jnp.sum(gathered[1:], axis=0), split(mat[...]))
        for q in range(NCH):
            kept_here[pl.ds(2 * q, 2), :] = part[0:2, q * W : (q + 1) * W]

    begin(shared)

    @on(1)
    def _():
        done(lbuf, rs.at[5])

    lower_high, lower_low = split(jnp.where(top, jnp.where(row_ids == lane_ids, -1.0, 0.0), lbuf[...].reshape(NB, NB)))

    checked[...] = few_rows(w8[...], (lower_high, lower_low))[0:2]
    begin(c5)
    multiplier = -bdot(jnp.concatenate([lower_low, lower_high, lower_high], axis=1), linv3[...])
    high, low_part = split(multiplier)
    factors[:, pl.ds(0, 3 * NB)] = jnp.concatenate([low_part, high, high], axis=1)

    for pair in PAIRS:
        for n in pair:
            done(esend.at[n], rd.at[n])
        for n in pair:
            cols = chunk_cols(n)
            got = slots[:, cols]
            got_high, got_low = split(got)
            high, low_part = split(jnp.where(owners[...] == prow, contrib[:, cols], got))
            rows_high[:, cols] = high
            rows_low[:, cols] = low_part
            product = bdot(factors[...], jnp.concatenate([high, low_part, high, got_low, got_high], axis=0))
            out_ref[:, cols] = mat[:, cols] * keep_col + product

    done(vbuf.at[1:], rs.at[8])
    u = jnp.concatenate([jnp.sum(vbuf[...], axis=0), jnp.zeros((6, NB), jnp.float32)], axis=0)
    check_factor = -few_rows(u, (linv3[pl.ds(0, NB), :], linv3[pl.ds(NB, NB), :]))

    done(sums.at[1:], rs.at[7])
    totals[...] = jnp.sum(sums[...], axis=0)
    checked_rows = few_rows(check_factor, (rows_high[...], rows_low[...]))
    for q in range(NCH):
        cols = pl.ds(q * W, W)
        chk_ref[:, cols] = checked_rows[0:2, q * W : (q + 1) * W] + totals[pl.ds(2 * q, 2), :]

    done(up1, ss.at[0])
    done(up2, ss.at[1])
    done(esend, ss.at[2])
    done(sums.at[1:], ss.at[7])
    done(vbuf.at[1:], ss.at[8])

    @on(1)
    def _():
        done(own_rows, ss.at[3])

    @on(0)
    def _():
        done(lbuf.at[1:], ss.at[4])
        done(lbuf, ss.at[5])

    @pl.when(prow != 0)
    def _():
        done(given, ss.at[6])


def hand_over(updated, checks, updated_out, checks_out, sems):
    size = NB // COPIES
    parts = [pl.ds(k * size, size) for k in range(COPIES)]
    copies = [pltpu.make_async_copy(updated.at[p], updated_out.at[p], sems.at[k]) for k, p in enumerate(parts)]
    copies.append(pltpu.make_async_copy(checks, checks_out, sems.at[COPIES]))
    for copy in copies:
        copy.start()
    for copy in copies:
        copy.wait()


def shards(nz, matrix, lpanel, linv, pivots, weights):
    f32 = jnp.float32
    columns = matrix.shape[1]
    n = NCH
    anywhere = pl.BlockSpec(memory_space=pl.ANY)
    vmem = pltpu.VMEM
    dma = pltpu.SemaphoreType.DMA
    operands = (matrix, lpanel, linv, pivots.reshape(1, NB), weights)
    updated, checks = pl.pallas_call(
        functools.partial(kernel, nz),
        out_shape=(vmem((NB, columns), f32), vmem((2, columns), f32)),
        in_specs=[anywhere] * 5,
        out_specs=(pl.BlockSpec(memory_space=vmem), pl.BlockSpec(memory_space=vmem)),
        scratch_shapes=[
            vmem((NB, columns), f32),
            vmem((NB, columns), f32),
            vmem((NB, NB), jnp.int32),
            vmem((2, NB, NB), jnp.int32),
            vmem((NB, NB), f32),
            vmem((1, NB), jnp.int32),
            vmem((8, NB), f32),
            vmem((8, NB), f32),
            vmem((nz, 2, 8, NB), f32),
            vmem((SIDE * SIDE, 2, NB), f32),
            vmem((n, 3, QUARTER, W), f32),
            vmem((n, QUARTER, W), f32),
            vmem((n, QUARTER, W), f32),
            vmem((n, 3, QUARTER, W), f32),
            vmem((n, 3, QUARTER, W), f32),
            vmem((NB, columns), f32),
            vmem((3 * NB, NB), jnp.bfloat16),
            vmem((NB + 16, 2 * NB), jnp.bfloat16),
            vmem((NB, 5 * NB), jnp.bfloat16),
            vmem((NB, columns), jnp.bfloat16),
            vmem((NB, columns), jnp.bfloat16),
            vmem((8, NB), f32),
            vmem((SIDE * SIDE, 8, NB), f32),
            vmem((SIDE * SIDE, 8, W), f32),
            vmem((8, W), f32),
            dma((4,)),
            dma((n,)),
            dma((n,)), dma((n,)), dma((n,)),
            dma((9,)), dma((9,)),
        ],
        compiler_params=pltpu.CompilerParams(
            collective_id=0, has_side_effects=True, vmem_limit_bytes=40 * 1024 * 1024
        ),
        cost_estimate=pl.CostEstimate(flops=500_000_000, bytes_accessed=4_000_000, transcendentals=0),
    )(*[pltpu.with_memory_space_constraint(v, pltpu.HBM) for v in operands])
    return pl.pallas_call(
        hand_over,
        out_shape=(
            jax.ShapeDtypeStruct((NB, columns), f32),
            jax.ShapeDtypeStruct((2, columns), f32),
        ),
        in_specs=[anywhere] * 2,
        out_specs=(anywhere, anywhere),
        scratch_shapes=[dma((COPIES + 1,))],
        cost_estimate=pl.CostEstimate(flops=0, bytes_accessed=2_000_000, transcendentals=0),
    )(*[pltpu.with_memory_space_constraint(v, vmem) for v in (updated, checks)])


def solution(mesh):
    return jax.shard_map(
        functools.partial(shards, mesh.shape["pcol"] // 2),
        mesh=mesh,
        in_specs=(P("prow", "pcol"), P(("prow", "pcol"), None), P(), P(), P(None, "prow")),
        out_specs=(P("prow", "pcol"), P(None, "pcol")),
        check_vma=False,
    )
```
